32 devices in a mesh: wide: 8 (over z, y), narrow: 4 (over x, core).
Axes of the slice: x: 2, y: 2, z: 4, core: 2. Of those that a mesh axis runs over, the one named last changes fastest.
Arguments:
- amplitudes: bfloat16 [3072, 8192], P(None, ('wide', 'narrow')), may hold values from -6 to 6
- integrals: bfloat16 [8192, 4096], P('wide', 'narrow'), may hold values from -0.0625 to 0.0625
- old_residual: float32 [3072, 4096], P('wide', 'narrow'), may hold values from -6 to 6
Outputs:
- new_residual: float32 [3072, 4096], P('wide', 'narrow')
The draws below stay inside these ranges and needn't reach their ends.
All inputs are finite; a program needn't handle non-finite values.
Results may differ from the reference program's by a relative error of at most 0.0003.
Values may be sent and summed in bfloat16 or wider, within the bound.
A program may use at most 128 MiB of HBM per device.

```python
import jax
import jax.numpy as jnp
from jax import lax

PAIRS_ROW = 384
PAIRS = 3072
CDPAIRS = 8192
ABPAIRS = 4096
N_WIDE = 8


def steps_of(own_key, dims, shards, smallest, high):
    def one(axis_at, blocks):
        steps = jax.random.uniform(jax.random.fold_in(jax.random.fold_in(own_key, 6), axis_at), (blocks,), jnp.float32, smallest / len(shards), high / len(shards))
        return jnp.repeat(jnp.exp(steps), dims[axis_at] // blocks).reshape((-1,) + (1,) * (len(dims) - axis_at - 1))

    factor_of = one(*shards[0])
    for cut in shards[1:]:
        factor_of = factor_of * one(*cut)
    return factor_of


def bell_draw(own_key, dims, width, limit, shards=(), held_as=jnp.bfloat16):
    entries = width * jax.random.normal(own_key, dims, jnp.float32)
    if shards:
        entries = entries * steps_of(own_key, dims, shards, -0.22, 0.18)
    return jnp.clip(entries, -limit, limit).astype(held_as)


def setup_inputs(seed: int = 0) -> dict:
    seeds = jax.random.split(jax.random.key(seed), 4)
    return {
        "amplitudes": bell_draw(seeds[0], (PAIRS, CDPAIRS), 1.0, 6.0, ((1, 32),)),
        "integrals": bell_draw(seeds[1], (CDPAIRS, ABPAIRS), CDPAIRS ** -0.5, 0.0625, ((0, 8), (1, 4))),
        "old_residual": bell_draw(seeds[2], (PAIRS, ABPAIRS), 1.0, 6.0, ((0, 8), (1, 4)), jnp.float32),
    }


def reference(amplitudes, integrals, old_residual):
    blocks = amplitudes.reshape(N_WIDE, PAIRS_ROW, amplitudes.shape[1])

    def one_block(block):
        return jnp.dot(block, integrals, preferred_element_type=jnp.float32)

    ladder = lax.map(one_block, blocks).reshape(old_residual.shape)
    return old_residual + ladder
```

```python
import functools

import jax
import jax.numpy as jnp
from jax import lax
from jax.experimental import pallas as pl
from jax.experimental.pallas import tpu as pltpu
from jax.sharding import PartitionSpec as P

WIRE = jnp.float32
CHUNKS = 4
MESH = pl.DeviceIdType.MESH


def kernel(nz, nc, a_ref, b_ref, r_ref, o_ref, a_all, b_all, part, send, up, dn,
           al_s, bl_s, ay_s, ay_r, ax_s, ax_r, ac_s, ac_r, by_s, by_r, z_s, up_r, dn_r):
    w, m = lax.axis_index("wide"), lax.axis_index("narrow")
    z, y, x, c = w // 2, w % 2, m // 2, m % 2
    rows, cols = r_ref.shape
    ka, kb = a_ref.shape[1], b_ref.shape[0]
    tile = cols // nc
    to_y = (z * 2 + 1 - y, m)
    to_x = (w, (1 - x) * 2 + c)
    to_c = (w, x * 2 + 1 - c)
    above, below = (w + 2, m), (w - 2, m)
    high = (2 * z) // nz

    def order(i):
        return i + (1 - high) * (nz - 1 - 2 * i)

    def piece(yy, xx, cc):
        return pl.ds(pl.multiple_of((yy * 4 + xx * 2 + cc) * ka, ka), ka)

    def rows_of(d, yy):
        return a_ref.at[pl.ds(pl.multiple_of((d * 2 + yy) * rows, rows), rows), :]

    def columns(n):
        return pl.ds(pl.multiple_of(n * tile, tile), tile)

    def remote(src, dst, s, r, to):
        return pltpu.make_async_remote_copy(
            src_ref=src, dst_ref=dst, send_sem=s, recv_sem=r, device_id=to, device_id_type=MESH)

    def a_local(i):
        d = order(i)
        return pltpu.make_async_copy(rows_of(d, y), a_all.at[d, :, piece(y, x, c)], al_s.at[i])

    def b_local(n):
        return pltpu.make_async_copy(
            b_ref.at[:, columns(n)], b_all.at[n, pl.ds(pl.multiple_of(y * kb, kb), kb)], bl_s.at[n])

    def a_y(i):
        d = order(i)
        return remote(rows_of(d, 1 - y), a_all.at[d, :, piece(y, x, c)], ay_s.at[i], ay_r.at[i], to_y)

    def a_x(i, j):
        d = order(i)
        src = rows_of(d, y) if j == 0 else a_all.at[d, :, piece(1 - y, x, c)]
        dst = a_all.at[d, :, piece(y if j == 0 else 1 - y, x, c)]
        return remote(src, dst, ax_s.at[i, j], ax_r.at[i, j], to_x)

    def a_c(i, j):
        d = order(i)
        here = piece(y if j % 2 == 0 else 1 - y, x if j < 2 else 1 - x, c)
        src = rows_of(d, y) if j == 0 else a_all.at[d, :, here]
        return remote(src, a_all.at[d, :, here], ac_s.at[i, j], ac_r.at[i, j], to_c)

    def b_y(n):
        return remote(b_ref.at[:, columns(n)], b_all.at[n, pl.ds(pl.multiple_of(y * kb, kb), kb)],
                      by_s.at[n], by_r.at[n], to_y)

    def c_up(d, n):
        return remote(send.at[d, n], up.at[d, n], z_s.at[d, n], up_r.at[d, n], above)

    def c_dn(d, n):
        return remote(send.at[d, n], dn.at[d, n], z_s.at[d, n], dn_r.at[d, n], below)

    for i in range(nz):
        a_local(i).start()
    for n in range(nc):
        b_local(n).start()

    barrier = pltpu.get_barrier_semaphore()
    for to in (to_y, to_x, to_c):
        pl.semaphore_signal(barrier, inc=1, device_id=to, device_id_type=MESH)

    @pl.when(z > 0)
    def _():
        pl.semaphore_signal(barrier, inc=1, device_id=below, device_id_type=MESH)

    @pl.when(z < nz - 1)
    def _():
        pl.semaphore_signal(barrier, inc=1, device_id=above, device_id_type=MESH)

    pl.semaphore_wait(barrier, 3 + (z + nz - 1) // nz + (2 * nz - 2 - z) // nz)

    def first(i):
        a_y(i).start()
        a_x(i, 0).start()
        a_c(i, 0).start()

    first(0)
    first(1)
    b_y(0).start()

    def step(t, carry):
        n, i = t // nz, t % nz
        d = order(i)

        @pl.when(n == 0)
        def _():
            a_y(i).wait_recv()
            a_x(i, 1).start()
            a_c(i, 1).start()

            @pl.when(i + 2 < nz)
            def _():
                first(i + 2)

            a_x(i, 0).wait_recv()
            a_c(i, 2).start()
            a_x(i, 1).wait_recv()
            a_c(i, 3).start()
            a_local(i).wait()
            for j in range(4):
                a_c(i, j).wait_recv()

        @pl.when(i == 0)
        def _():
            @pl.when(n + 1 < nc)
            def _():
                b_y(n + 1).start()

            b_local(n).wait()
            b_y(n).wait_recv()

        part[...] = jnp.dot(a_all[d], b_all[n], preferred_element_type=jnp.float32)

        @pl.when(d == z)
        def _():
            o_ref[:, columns(n)] = r_ref[:, columns(n)] + part[...]

        @pl.when(d > z)
        def _():
            @pl.when(z > 0)
            def _():
                c_up(d, n).wait_recv()
                send[d, n] = (part[...] + up[d, n].astype(jnp.float32)).astype(send.dtype)

            @pl.when(z == 0)
            def _():
                send[d, n] = part[...].astype(send.dtype)

            c_up(d, n).start()

        @pl.when(d < z)
        def _():
            @pl.when(z < nz - 1)
            def _():
                c_dn(d, n).wait_recv()
                send[d, n] = (part[...] + dn[d, n].astype(jnp.float32)).astype(send.dtype)

            @pl.when(z == nz - 1)
            def _():
                send[d, n] = part[...].astype(send.dtype)

            c_dn(d, n).start()

        return carry

    lax.fori_loop(0, nz * nc, step, 0)

    def finish(n, carry):
        @pl.when(z > 0)
        def _():
            c_up(z, n).wait_recv()
            o_ref[:, columns(n)] += up[z, n].astype(jnp.float32)

        @pl.when(z < nz - 1)
        def _():
            c_dn(z, n).wait_recv()
            o_ref[:, columns(n)] += dn[z, n].astype(jnp.float32)

        return carry

    lax.fori_loop(0, nc, finish, 0)

    def drain_a(i, carry):
        a_y(i).wait_send()
        for j in range(2):
            a_x(i, j).wait_send()
        for j in range(4):
            a_c(i, j).wait_send()
        return carry

    def drain_b(n, carry):
        b_y(n).wait_send()
        return carry

    def drain_c(t, carry):
        d, n = t // nc, t % nc

        @pl.when(d != z)
        def _():
            c_up(d, n).wait_send()

        return carry

    lax.fori_loop(0, nz, drain_a, 0)
    lax.fori_loop(0, nc, drain_b, 0)
    lax.fori_loop(0, nz * nc, drain_c, 0)


def ladder_kernel(amplitudes, integrals, old_residual):
    nz, nc = lax.axis_size("wide") // 2, CHUNKS
    rows, cols = old_residual.shape
    depth = 2 * integrals.shape[0]
    tile = cols // nc
    dma = pltpu.SemaphoreType.DMA
    return pl.pallas_call(
        functools.partial(kernel, nz, nc),
        out_shape=jax.ShapeDtypeStruct((rows, cols), jnp.float32),
        in_specs=[pl.BlockSpec(memory_space=pl.ANY)] * 2 + [pl.BlockSpec(memory_space=pltpu.VMEM)],
        out_specs=pl.BlockSpec(memory_space=pltpu.VMEM),
        scratch_shapes=[
            pltpu.VMEM((nz, rows, depth), jnp.bfloat16),
            pltpu.VMEM((nc, depth, tile), jnp.bfloat16),
            pltpu.VMEM((rows, tile), jnp.float32),
            pltpu.VMEM((nz, nc, rows, tile), WIRE),
            pltpu.VMEM((nz, nc, rows, tile), WIRE),
            pltpu.VMEM((nz, nc, rows, tile), WIRE),
            dma((nz,)), dma((nc,)),
            dma((nz,)), dma((nz,)),
            dma((nz, 2)), dma((nz, 2)),
            dma((nz, 4)), dma((nz, 4)),
            dma((nc,)), dma((nc,)),
            dma((nz, nc)), dma((nz, nc)), dma((nz, nc)),
        ],
        compiler_params=pltpu.CompilerParams(
            collective_id=0, has_side_effects=True, vmem_limit_bytes=50 * 1024 * 1024),
        cost_estimate=pl.CostEstimate(
            flops=2 * nz * rows * depth * cols, bytes_accessed=8 * rows * cols, transcendentals=0),
    )(amplitudes, integrals, old_residual)


def broadcast(value, axis, source):
    kept = jnp.where(lax.axis_index(axis) == source, value, 0).astype(value.dtype)
    return lax.psum(kept, axis)


def ladder_gathered(amplitudes, integrals, old_residual):
    panels = lax.axis_size("narrow")
    sub_rows = integrals.shape[0] // panels
    stacked = integrals.reshape(panels, sub_rows, integrals.shape[1])
    total = old_residual
    row_amps = lax.all_to_all(amplitudes, "wide", split_axis=0, concat_axis=1, tiled=True)
    for column in range(panels):
        panel = broadcast(row_amps, "narrow", column)
        panel_ints = lax.all_gather(stacked[column], "wide", axis=0, tiled=True)
        total = total + jnp.dot(panel, panel_ints, preferred_element_type=jnp.float32)
    return total


def per_device(amplitudes, integrals, old_residual):
    if amplitudes.shape[1] % 128 or lax.axis_size("narrow") != 4 or lax.axis_size("wide") > 8:
        return ladder_gathered(amplitudes, integrals, old_residual)
    return ladder_kernel(amplitudes, integrals, old_residual)


def solution(mesh):
    placed = (P(None, ("wide", "narrow")), P("wide", "narrow"), P("wide", "narrow"))
    return jax.shard_map(
        per_device, mesh=mesh, in_specs=placed, out_specs=P("wide", "narrow"), check_vma=False
    )
```

```python
import functools

import jax
import jax.numpy as jnp
from jax import lax
from jax.experimental import pallas as pl
from jax.experimental.pallas import tpu as pltpu
from jax.sharding import PartitionSpec as P

SCALE_ROWS = 16
KEEP = 46000.0
CHUNKS = 4
MESH = pl.DeviceIdType.MESH


def encode(ref, d, n, value):
    rows = value.shape[0]
    peak = jnp.max(jnp.abs(value), axis=0, keepdims=True)
    scale = (peak * 1.01 + 1e-30).astype(jnp.bfloat16)
    q = value * (KEEP / scale.astype(jnp.float32))
    q2 = q * q
    q4 = q2 * q2
    ref[d, n, :rows] = (q4 * q2 * (q * jnp.abs(q))).astype(jnp.bfloat16)
    ref[d, n, rows:] = jnp.broadcast_to(scale, (SCALE_ROWS, value.shape[1]))


def decode(ref, d, n, rows):
    code = ref[d, n, :rows].astype(jnp.float32)
    scale = ref[d, n, rows:].astype(jnp.float32)[:1]
    r1 = lax.rsqrt(jnp.maximum(jnp.abs(code), 1.2e-38))
    r2 = lax.rsqrt(r1)
    root = r2 * lax.rsqrt(r2)
    return jnp.where(code < 0, -root, root) * (scale * (1.0 / KEEP))


def kernel(nz, nc, a_ref, b_ref, r_ref, o_ref, a_all, b_all, part, send, up, dn,
           al_s, bl_s, ay_s, ay_r, ax_s, ax_r, ac_s, ac_r, by_s, by_r, z_s, up_r, dn_r):
    w, m = lax.axis_index("wide"), lax.axis_index("narrow")
    z, y, x, c = w // 2, w % 2, m // 2, m % 2
    rows, cols = r_ref.shape
    ka, kb = a_ref.shape[1], b_ref.shape[0]
    tile = cols // nc
    to_y = (z * 2 + 1 - y, m)
    to_x = (w, (1 - x) * 2 + c)
    to_c = (w, x * 2 + 1 - c)
    above, below = (w + 2, m), (w - 2, m)
    high = (2 * z) // nz

    def order(i):
        return i + (1 - high) * (nz - 1 - 2 * i)

    def piece(yy, xx, cc):
        return pl.ds(pl.multiple_of((yy * 4 + xx * 2 + cc) * ka, ka), ka)

    def rows_of(d, yy):
        return a_ref.at[pl.ds(pl.multiple_of((d * 2 + yy) * rows, rows), rows), :]

    def columns(n):
        return pl.ds(pl.multiple_of(n * tile, tile), tile)

    def remote(src, dst, s, r, to):
        return pltpu.make_async_remote_copy(
            src_ref=src, dst_ref=dst, send_sem=s, recv_sem=r, device_id=to, device_id_type=MESH)

    def a_local(i):
        d = order(i)
        return pltpu.make_async_copy(rows_of(d, y), a_all.at[d, :, piece(y, x, c)], al_s.at[i])

    def b_local(n):
        return pltpu.make_async_copy(
            b_ref.at[:, columns(n)], b_all.at[n, pl.ds(pl.multiple_of(y * kb, kb), kb)], bl_s.at[n])

    def a_y(i):
        d = order(i)
        return remote(rows_of(d, 1 - y), a_all.at[d, :, piece(y, x, c)], ay_s.at[i], ay_r.at[i], to_y)

    def a_x(i, j):
        d = order(i)
        src = rows_of(d, y) if j == 0 else a_all.at[d, :, piece(1 - y, x, c)]
        dst = a_all.at[d, :, piece(y if j == 0 else 1 - y, x, c)]
        return remote(src, dst, ax_s.at[i, j], ax_r.at[i, j], to_x)

    def a_c(i, j):
        d = order(i)
        here = piece(y if j % 2 == 0 else 1 - y, x if j < 2 else 1 - x, c)
        src = rows_of(d, y) if j == 0 else a_all.at[d, :, here]
        return remote(src, a_all.at[d, :, here], ac_s.at[i, j], ac_r.at[i, j], to_c)

    def b_y(n):
        return remote(b_ref.at[:, columns(n)], b_all.at[n, pl.ds(pl.multiple_of(y * kb, kb), kb)],
                      by_s.at[n], by_r.at[n], to_y)

    def c_up(d, n):
        return remote(send.at[d, n], up.at[d, n], z_s.at[d, n], up_r.at[d, n], above)

    def c_dn(d, n):
        return remote(send.at[d, n], dn.at[d, n], z_s.at[d, n], dn_r.at[d, n], below)

    for i in range(nz):
        a_local(i).start()
    for n in range(nc):
        b_local(n).start()

    barrier = pltpu.get_barrier_semaphore()
    for to in (to_y, to_x, to_c):
        pl.semaphore_signal(barrier, inc=1, device_id=to, device_id_type=MESH)

    @pl.when(z > 0)
    def _():
        pl.semaphore_signal(barrier, inc=1, device_id=below, device_id_type=MESH)

    @pl.when(z < nz - 1)
    def _():
        pl.semaphore_signal(barrier, inc=1, device_id=above, device_id_type=MESH)

    pl.semaphore_wait(barrier, 3 + (z + nz - 1) // nz + (2 * nz - 2 - z) // nz)

    def first(i):
        a_y(i).start()
        a_x(i, 0).start()
        a_c(i, 0).start()

    first(0)
    first(1)
    b_y(0).start()

    def step(t, carry):
        n, i = t // nz, t % nz
        d = order(i)

        @pl.when(n == 0)
        def _():
            a_y(i).wait_recv()
            a_x(i, 1).start()
            a_c(i, 1).start()

            @pl.when(i + 2 < nz)
            def _():
                first(i + 2)

            a_x(i, 0).wait_recv()
            a_c(i, 2).start()
            a_x(i, 1).wait_recv()
            a_c(i, 3).start()
            a_local(i).wait()
            for j in range(4):
                a_c(i, j).wait_recv()

        @pl.when(i == 0)
        def _():
            @pl.when(n + 1 < nc)
            def _():
                b_y(n + 1).start()

            b_local(n).wait()
            b_y(n).wait_recv()

        part[...] = jnp.dot(a_all[d], b_all[n], preferred_element_type=jnp.float32)

        @pl.when(d == z)
        def _():
            o_ref[:, columns(n)] = r_ref[:, columns(n)] + part[...]

        @pl.when(d > z)
        def _():
            @pl.when(z > 0)
            def _():
                c_up(d, n).wait_recv()
                encode(send, d, n, part[...] + decode(up, d, n, rows))

            @pl.when(z == 0)
            def _():
                encode(send, d, n, part[...])

            c_up(d, n).start()

        @pl.when(d < z)
        def _():
            @pl.when(z < nz - 1)
            def _():
                c_dn(d, n).wait_recv()
                encode(send, d, n, part[...] + decode(dn, d, n, rows))

            @pl.when(z == nz - 1)
            def _():
                encode(send, d, n, part[...])

            c_dn(d, n).start()

        return carry

    lax.fori_loop(0, nz * nc, step, 0)

    def finish(n, carry):
        @pl.when(z > 0)
        def _():
            c_up(z, n).wait_recv()
            o_ref[:, columns(n)] += decode(up, z, n, rows)

        @pl.when(z < nz - 1)
        def _():
            c_dn(z, n).wait_recv()
            o_ref[:, columns(n)] += decode(dn, z, n, rows)

        return carry

    lax.fori_loop(0, nc, finish, 0)

    def drain_a(i, carry):
        a_y(i).wait_send()
        for j in range(2):
            a_x(i, j).wait_send()
        for j in range(4):
            a_c(i, j).wait_send()
        return carry

    def drain_b(n, carry):
        b_y(n).wait_send()
        return carry

    def drain_c(t, carry):
        d, n = t // nc, t % nc

        @pl.when(d != z)
        def _():
            c_up(d, n).wait_send()

        return carry

    lax.fori_loop(0, nz, drain_a, 0)
    lax.fori_loop(0, nc, drain_b, 0)
    lax.fori_loop(0, nz * nc, drain_c, 0)


def ladder_kernel(amplitudes, integrals, old_residual):
    nz, nc = lax.axis_size("wide") // 2, CHUNKS
    rows, cols = old_residual.shape
    depth = 2 * integrals.shape[0]
    tile = cols // nc
    dma = pltpu.SemaphoreType.DMA
    return pl.pallas_call(
        functools.partial(kernel, nz, nc),
        out_shape=jax.ShapeDtypeStruct((rows, cols), jnp.float32),
        in_specs=[pl.BlockSpec(memory_space=pl.ANY)] * 2 + [pl.BlockSpec(memory_space=pltpu.VMEM)],
        out_specs=pl.BlockSpec(memory_space=pltpu.VMEM),
        scratch_shapes=[
            pltpu.VMEM((nz, rows, depth), jnp.bfloat16),
            pltpu.VMEM((nc, depth, tile), jnp.bfloat16),
            pltpu.VMEM((rows, tile), jnp.float32),
            pltpu.VMEM((nz, nc, rows + SCALE_ROWS, tile), jnp.bfloat16),
            pltpu.VMEM((nz, nc, rows + SCALE_ROWS, tile), jnp.bfloat16),
            pltpu.VMEM((nz, nc, rows + SCALE_ROWS, tile), jnp.bfloat16),
            dma((nz,)), dma((nc,)),
            dma((nz,)), dma((nz,)),
            dma((nz, 2)), dma((nz, 2)),
            dma((nz, 4)), dma((nz, 4)),
            dma((nc,)), dma((nc,)),
            dma((nz, nc)), dma((nz, nc)), dma((nz, nc)),
        ],
        compiler_params=pltpu.CompilerParams(
            collective_id=0, has_side_effects=True, vmem_limit_bytes=50 * 1024 * 1024),
        cost_estimate=pl.CostEstimate(
            flops=2 * nz * rows * depth * cols, bytes_accessed=8 * rows * cols, transcendentals=0),
    )(amplitudes, integrals, old_residual)


def broadcast(value, axis, source):
    kept = jnp.where(lax.axis_index(axis) == source, value, 0).astype(value.dtype)
    return lax.psum(kept, axis)


def ladder_gathered(amplitudes, integrals, old_residual):
    panels = lax.axis_size("narrow")
    sub_rows = integrals.shape[0] // panels
    stacked = integrals.reshape(panels, sub_rows, integrals.shape[1])
    total = old_residual
    row_amps = lax.all_to_all(amplitudes, "wide", split_axis=0, concat_axis=1, tiled=True)
    for column in range(panels):
        panel = broadcast(row_amps, "narrow", column)
        panel_ints = lax.all_gather(stacked[column], "wide", axis=0, tiled=True)
        total = total + jnp.dot(panel, panel_ints, preferred_element_type=jnp.float32)
    return total


def per_device(amplitudes, integrals, old_residual):
    if amplitudes.shape[1] % 128 or lax.axis_size("narrow") != 4 or lax.axis_size("wide") > 8:
        return ladder_gathered(amplitudes, integrals, old_residual)
    return ladder_kernel(amplitudes, integrals, old_residual)


def solution(mesh):
    placed = (P(None, ("wide", "narrow")), P("wide", "narrow"), P("wide", "narrow"))
    return jax.shard_map(
        per_device, mesh=mesh, in_specs=placed, out_specs=P("wide", "narrow"), check_vma=False
    )
```

```python
import functools

import jax
import jax.numpy as jnp
from jax import lax
from jax.experimental import pallas as pl
from jax.experimental.pallas import tpu as pltpu
from jax.sharding import PartitionSpec as P

SCALE_ROWS = 16
KEEP = 46000.0
CHUNKS = 8
MESH = pl.DeviceIdType.MESH


def encode(ref, d, n, value):
    rows = value.shape[0]
    peak = jnp.max(jnp.abs(value), axis=0, keepdims=True)
    scale = (peak * 1.01 + 1e-30).astype(jnp.bfloat16)
    q = value * (KEEP / scale.astype(jnp.float32))
    q2 = q * q
    q4 = q2 * q2
    ref[d, n, :rows] = (q4 * q2 * (q * jnp.abs(q))).astype(jnp.bfloat16)
    ref[d, n, rows:] = jnp.broadcast_to(scale, (SCALE_ROWS, value.shape[1]))


def decode(ref, d, n, rows):
    code = ref[d, n, :rows].astype(jnp.float32)
    scale = ref[d, n, rows:].astype(jnp.float32)[:1]
    r1 = lax.rsqrt(jnp.maximum(jnp.abs(code), 1.2e-38))
    r2 = lax.rsqrt(r1)
    root = r2 * lax.rsqrt(r2)
    return jnp.where(code < 0, -root, root) * (scale * (1.0 / KEEP))


def kernel(nz, nc, a_ref, b_ref, r_ref, o_ref, a_all, b_all, part, send, up, dn,
           r_s, al_s, bl_s, ay_s, ay_r, ax_s, ax_r, ac_s, ac_r, by_s, by_r, z_s, up_r, dn_r):
    w, m = lax.axis_index("wide"), lax.axis_index("narrow")
    z, y, x, c = w // 2, w % 2, m // 2, m % 2
    rows, cols = r_ref.shape
    ka, kb = a_ref.shape[1], b_ref.shape[0]
    tile = cols // nc
    to_y = (z * 2 + 1 - y, m)
    to_x = (w, (1 - x) * 2 + c)
    to_c = (w, x * 2 + 1 - c)
    above, below = (w + 2, m), (w - 2, m)
    high = (2 * z) // nz

    def order(i):
        return i + (1 - high) * (nz - 1 - 2 * i)

    def piece(yy, xx, cc):
        return pl.ds(pl.multiple_of((yy * 4 + xx * 2 + cc) * ka, ka), ka)

    def rows_of(d, yy):
        return a_ref.at[pl.ds(pl.multiple_of((d * 2 + yy) * rows, rows), rows), :]

    def columns(n):
        return pl.ds(pl.multiple_of(n * tile, tile), tile)

    def remote(src, dst, s, r, to):
        return pltpu.make_async_remote_copy(
            src_ref=src, dst_ref=dst, send_sem=s, recv_sem=r, device_id=to, device_id_type=MESH)

    def a_local(i):
        d = order(i)
        return pltpu.make_async_copy(rows_of(d, y), a_all.at[d, :, piece(y, x, c)], al_s.at[i])

    def b_local(n):
        return pltpu.make_async_copy(
            b_ref.at[:, columns(n)], b_all.at[n, pl.ds(pl.multiple_of(y * kb, kb), kb)], bl_s.at[n])

    def a_y(i):
        d = order(i)
        return remote(rows_of(d, 1 - y), a_all.at[d, :, piece(y, x, c)], ay_s.at[i], ay_r.at[i], to_y)

    def a_x(i, j):
        d = order(i)
        src = rows_of(d, y) if j == 0 else a_all.at[d, :, piece(1 - y, x, c)]
        dst = a_all.at[d, :, piece(y if j == 0 else 1 - y, x, c)]
        return remote(src, dst, ax_s.at[i, j], ax_r.at[i, j], to_x)

    def a_c(i, j):
        d = order(i)
        here = piece(y if j % 2 == 0 else 1 - y, x if j < 2 else 1 - x, c)
        src = rows_of(d, y) if j == 0 else a_all.at[d, :, here]
        return remote(src, a_all.at[d, :, here], ac_s.at[i, j], ac_r.at[i, j], to_c)

    def b_y(n):
        return remote(b_ref.at[:, columns(n)], b_all.at[n, pl.ds(pl.multiple_of(y * kb, kb), kb)],
                      by_s.at[n], by_r.at[n], to_y)

    def c_up(d, n):
        return remote(send.at[d, n], up.at[d, n], z_s.at[d, n], up_r.at[d, n], above)

    def c_dn(d, n):
        return remote(send.at[d, n], dn.at[d, n], z_s.at[d, n], dn_r.at[d, n], below)

    residual = pltpu.make_async_copy(r_ref, o_ref, r_s)
    for i in range(nz):
        a_local(i).start()
    for n in range(nc):
        b_local(n).start()
    residual.start()

    barrier = pltpu.get_barrier_semaphore()
    for to in (to_y, to_x, to_c):
        pl.semaphore_signal(barrier, inc=1, device_id=to, device_id_type=MESH)

    @pl.when(z > 0)
    def _():
        pl.semaphore_signal(barrier, inc=1, device_id=below, device_id_type=MESH)

    @pl.when(z < nz - 1)
    def _():
        pl.semaphore_signal(barrier, inc=1, device_id=above, device_id_type=MESH)

    pl.semaphore_wait(barrier, 3 + (z + nz - 1) // nz + (2 * nz - 2 - z) // nz)

    def first(i):
        a_y(i).start()
        a_x(i, 0).start()
        a_c(i, 0).start()

    first(0)
    first(1)
    b_y(0).start()
    residual.wait()

    def step(t, carry):
        n, i = t // nz, t % nz
        d = order(i)

        @pl.when(n == 0)
        def _():
            a_y(i).wait_recv()
            a_x(i, 1).start()
            a_c(i, 1).start()

            @pl.when(i + 2 < nz)
            def _():
                first(i + 2)

            a_x(i, 0).wait_recv()
            a_c(i, 2).start()
            a_x(i, 1).wait_recv()
            a_c(i, 3).start()
            a_local(i).wait()
            for j in range(4):
                a_c(i, j).wait_recv()

        @pl.when(i == 0)
        def _():
            @pl.when(n + 1 < nc)
            def _():
                b_y(n + 1).start()

            b_local(n).wait()
            b_y(n).wait_recv()

        part[...] = jnp.dot(a_all[d], b_all[n], preferred_element_type=jnp.float32)

        @pl.when(d == z)
        def _():
            o_ref[:, columns(n)] += part[...]

        @pl.when(d > z)
        def _():
            @pl.when(z > 0)
            def _():
                c_up(d, n).wait_recv()
                encode(send, d, n, part[...] + decode(up, d, n, rows))

            @pl.when(z == 0)
            def _():
                encode(send, d, n, part[...])

            c_up(d, n).start()

        @pl.when(d < z)
        def _():
            @pl.when(z < nz - 1)
            def _():
                c_dn(d, n).wait_recv()
                encode(send, d, n, part[...] + decode(dn, d, n, rows))

            @pl.when(z == nz - 1)
            def _():
                encode(send, d, n, part[...])

            c_dn(d, n).start()

        return carry

    lax.fori_loop(0, nz * nc, step, 0)

    def finish(n, carry):
        @pl.when(z > 0)
        def _():
            c_up(z, n).wait_recv()
            o_ref[:, columns(n)] += decode(up, z, n, rows)

        @pl.when(z < nz - 1)
        def _():
            c_dn(z, n).wait_recv()
            o_ref[:, columns(n)] += decode(dn, z, n, rows)

        return carry

    lax.fori_loop(0, nc, finish, 0)

    def drain_a(i, carry):
        a_y(i).wait_send()
        for j in range(2):
            a_x(i, j).wait_send()
        for j in range(4):
            a_c(i, j).wait_send()
        return carry

    def drain_b(n, carry):
        b_y(n).wait_send()
        return carry

    def drain_c(t, carry):
        d, n = t // nc, t % nc

        @pl.when(d != z)
        def _():
            c_up(d, n).wait_send()

        return carry

    lax.fori_loop(0, nz, drain_a, 0)
    lax.fori_loop(0, nc, drain_b, 0)
    lax.fori_loop(0, nz * nc, drain_c, 0)


def ladder_kernel(amplitudes, integrals, old_residual):
    nz, nc = lax.axis_size("wide") // 2, CHUNKS
    rows, cols = old_residual.shape
    depth = 2 * integrals.shape[0]
    tile = cols // nc
    dma = pltpu.SemaphoreType.DMA
    return pl.pallas_call(
        functools.partial(kernel, nz, nc),
        out_shape=jax.ShapeDtypeStruct((rows, cols), jnp.float32),
        in_specs=[pl.BlockSpec(memory_space=pl.ANY)] * 3,
        out_specs=pl.BlockSpec(memory_space=pltpu.VMEM),
        scratch_shapes=[
            pltpu.VMEM((nz, rows, depth), jnp.bfloat16),
            pltpu.VMEM((nc, depth, tile), jnp.bfloat16),
            pltpu.VMEM((rows, tile), jnp.float32),
            pltpu.VMEM((nz, nc, rows + SCALE_ROWS, tile), jnp.bfloat16),
            pltpu.VMEM((nz, nc, rows + SCALE_ROWS, tile), jnp.bfloat16),
            pltpu.VMEM((nz, nc, rows + SCALE_ROWS, tile), jnp.bfloat16),
            dma, dma((nz,)), dma((nc,)),
            dma((nz,)), dma((nz,)),
            dma((nz, 2)), dma((nz, 2)),
            dma((nz, 4)), dma((nz, 4)),
            dma((nc,)), dma((nc,)),
            dma((nz, nc)), dma((nz, nc)), dma((nz, nc)),
        ],
        compiler_params=pltpu.CompilerParams(
            collective_id=0, has_side_effects=True, vmem_limit_bytes=50 * 1024 * 1024),
        cost_estimate=pl.CostEstimate(
            flops=2 * nz * rows * depth * cols, bytes_accessed=8 * rows * cols, transcendentals=0),
    )(amplitudes, integrals, old_residual)


def broadcast(value, axis, source):
    kept = jnp.where(lax.axis_index(axis) == source, value, 0).astype(value.dtype)
    return lax.psum(kept, axis)


def ladder_gathered(amplitudes, integrals, old_residual):
    panels = lax.axis_size("narrow")
    sub_rows = integrals.shape[0] // panels
    stacked = integrals.reshape(panels, sub_rows, integrals.shape[1])
    total = old_residual
    row_amps = lax.all_to_all(amplitudes, "wide", split_axis=0, concat_axis=1, tiled=True)
    for column in range(panels):
        panel = broadcast(row_amps, "narrow", column)
        panel_ints = lax.all_gather(stacked[column], "wide", axis=0, tiled=True)
        total = total + jnp.dot(panel, panel_ints, preferred_element_type=jnp.float32)
    return total


def per_device(amplitudes, integrals, old_residual):
    if amplitudes.shape[1] % 128 or lax.axis_size("narrow") != 4 or lax.axis_size("wide") > 8:
        return ladder_gathered(amplitudes, integrals, old_residual)
    return ladder_kernel(amplitudes, integrals, old_residual)


def solution(mesh):
    placed = (P(None, ("wide", "narrow")), P("wide", "narrow"), P("wide", "narrow"))
    return jax.shard_map(
        per_device, mesh=mesh, in_specs=placed, out_specs=P("wide", "narrow"), check_vma=False
    )
```

```python
import functools

import jax
import jax.numpy as jnp
from jax import lax
from jax.experimental import pallas as pl
from jax.experimental.pallas import tpu as pltpu
from jax.sharding import PartitionSpec as P

SCALE_ROWS = 16
KEEP = 46000.0
CHUNKS = 8
AHEAD = 3
MESH = pl.DeviceIdType.MESH


def encode(ref, d, n, value):
    rows = value.shape[0]
    peak = jnp.max(jnp.abs(value), axis=0, keepdims=True)
    scale = (peak * 1.01 + 1e-30).astype(jnp.bfloat16)
    q = value * (KEEP / scale.astype(jnp.float32))
    q2 = q * q
    q4 = q2 * q2
    ref[d, n, :rows] = (q4 * q2 * (q * jnp.abs(q))).astype(jnp.bfloat16)
    ref[d, n, rows:] = jnp.broadcast_to(scale, (SCALE_ROWS, value.shape[1]))


def decode(ref, d, n, rows):
    code = ref[d, n, :rows].astype(jnp.float32)
    scale = ref[d, n, rows:].astype(jnp.float32)[:1]
    r1 = lax.rsqrt(jnp.maximum(jnp.abs(code), 1.2e-38))
    r2 = lax.rsqrt(r1)
    root = r2 * lax.rsqrt(r2)
    return jnp.where(code < 0, -root, root) * (scale * (1.0 / KEEP))


def kernel(nz, nc, a_ref, b_ref, r_ref, o_ref, a_all, b_all, part, send, up, dn,
           r_s, al_s, bl_s, ay_s, ay_r, ax_s, ax_r, ac_s, ac_r, by_s, by_r, z_s, up_r, dn_r):
    w, m = lax.axis_index("wide"), lax.axis_index("narrow")
    z, y, x, c = w // 2, w % 2, m // 2, m % 2
    rows, cols = r_ref.shape
    ka, kb = a_ref.shape[1], b_ref.shape[0]
    tile = cols // nc
    to_y = (z * 2 + 1 - y, m)
    to_x = (w, (1 - x) * 2 + c)
    to_c = (w, x * 2 + 1 - c)
    above, below = (w + 2, m), (w - 2, m)
    high = (2 * z) // nz

    own = z + (1 - high) * (nz - 1 - 2 * z)

    def order(i):
        last = (i + 1) // nz
        k = last * own + (1 - last) * (i + (i + nz - own) // nz)
        return k + (1 - high) * (nz - 1 - 2 * k)

    def piece(yy, xx, cc):
        return pl.ds(pl.multiple_of((yy * 4 + xx * 2 + cc) * ka, ka), ka)

    def rows_of(d, yy):
        return a_ref.at[pl.ds(pl.multiple_of((d * 2 + yy) * rows, rows), rows), :]

    def columns(n):
        return pl.ds(pl.multiple_of(n * tile, tile), tile)

    def remote(src, dst, s, r, to):
        return pltpu.make_async_remote_copy(
            src_ref=src, dst_ref=dst, send_sem=s, recv_sem=r, device_id=to, device_id_type=MESH)

    def a_local(i):
        d = order(i)
        return pltpu.make_async_copy(rows_of(d, y), a_all.at[d, :, piece(y, x, c)], al_s.at[i])

    def b_local(n):
        return pltpu.make_async_copy(
            b_ref.at[:, columns(n)], b_all.at[n, pl.ds(pl.multiple_of(y * kb, kb), kb)], bl_s.at[n])

    def a_y(i):
        d = order(i)
        return remote(rows_of(d, 1 - y), a_all.at[d, :, piece(y, x, c)], ay_s.at[i], ay_r.at[i], to_y)

    def a_x(i, j):
        d = order(i)
        src = rows_of(d, y) if j == 0 else a_all.at[d, :, piece(1 - y, x, c)]
        dst = a_all.at[d, :, piece(y if j == 0 else 1 - y, x, c)]
        return remote(src, dst, ax_s.at[i, j], ax_r.at[i, j], to_x)

    def a_c(i, j):
        d = order(i)
        here = piece(y if j % 2 == 0 else 1 - y, x if j < 2 else 1 - x, c)
        src = rows_of(d, y) if j == 0 else a_all.at[d, :, here]
        return remote(src, a_all.at[d, :, here], ac_s.at[i, j], ac_r.at[i, j], to_c)

    def b_y(n):
        return remote(b_ref.at[:, columns(n)], b_all.at[n, pl.ds(pl.multiple_of(y * kb, kb), kb)],
                      by_s.at[n], by_r.at[n], to_y)

    def c_up(d, n):
        return remote(send.at[d, n], up.at[d, n], z_s.at[d, n], up_r.at[d, n], above)

    def c_dn(d, n):
        return remote(send.at[d, n], dn.at[d, n], z_s.at[d, n], dn_r.at[d, n], below)

    residual = pltpu.make_async_copy(r_ref, o_ref, r_s)
    for i in range(nz):
        a_local(i).start()
    for n in range(nc):
        b_local(n).start()
    residual.start()

    barrier = pltpu.get_barrier_semaphore()
    for to in (to_y, to_x, to_c):
        pl.semaphore_signal(barrier, inc=1, device_id=to, device_id_type=MESH)

    @pl.when(z > 0)
    def _():
        pl.semaphore_signal(barrier, inc=1, device_id=below, device_id_type=MESH)

    @pl.when(z < nz - 1)
    def _():
        pl.semaphore_signal(barrier, inc=1, device_id=above, device_id_type=MESH)

    pl.semaphore_wait(barrier, 3 + (z + nz - 1) // nz + (2 * nz - 2 - z) // nz)

    queue = []
    for e in range(nz - 1):
        queue += [("a", e), ("b", e)]
    queue += [("b", n) for n in range(nz - 1, nc - 1)] + [("a", nz - 1), ("b", nc - 1)]

    def start_y(k):
        if k < len(queue):
            (a_y if queue[k][0] == "a" else b_y)(queue[k][1]).start()

    def start_own(i):
        if i < nz:
            a_x(i, 0).start()
            a_c(i, 0).start()

    def a_arrives(i):
        a_y(i).wait_recv()
        start_y(queue.index(("a", i)) + AHEAD)
        a_x(i, 1).start()
        a_c(i, 1).start()
        start_own(i + 2)

    def b_arrives(n):
        b_local(n).wait()
        b_y(n).wait_recv()
        start_y(queue.index(("b", n)) + AHEAD)

    def a_complete(i):
        a_x(i, 0).wait_recv()
        a_c(i, 2).start()
        a_x(i, 1).wait_recv()
        a_c(i, 3).start()
        a_local(i).wait()
        for j in range(4):
            a_c(i, j).wait_recv()

    for k in range(AHEAD):
        start_y(k)
    start_own(0)
    start_own(1)
    residual.wait()

    head = [(0, 0)]
    for e in range(1, nz - 1):
        head += [(i, e) for i in range(e)] + [(e, n) for n in range(e + 1)]
    sends = (nz - 1) * nc

    def step(t, carry):
        i = (t - len(head)) % (nz - 1)
        n = nz - 1 + (t - len(head)) // (nz - 1)
        for k, (head_i, head_n) in enumerate(head):
            i = jnp.where(t == k, head_i, i)
            n = jnp.where(t == k, head_n, n)
        d = order(i)

        @pl.when(t == 0)
        def _():
            a_arrives(0)
            b_arrives(0)
            a_complete(0)

        for e in range(1, nz - 1):
            @pl.when(t == head.index((0, e)))
            def _():
                a_arrives(e)
                b_arrives(e)

            @pl.when(t == head.index((e, 0)))
            def _():
                a_complete(e)

        for e in range(nz - 1, nc):
            @pl.when(t == len(head) + (e - nz + 1) * (nz - 1))
            def _():
                if e == nc - 1:
                    a_arrives(nz - 1)
                b_arrives(e)

        part[...] = jnp.dot(a_all[d], b_all[n], preferred_element_type=jnp.float32)

        @pl.when(d > z)
        def _():
            @pl.when(z > 0)
            def _():
                c_up(d, n).wait_recv()
                encode(send, d, n, part[...] + decode(up, d, n, rows))

            @pl.when(z == 0)
            def _():
                encode(send, d, n, part[...])

            c_up(d, n).start()

        @pl.when(d < z)
        def _():
            @pl.when(z < nz - 1)
            def _():
                c_dn(d, n).wait_recv()
                encode(send, d, n, part[...] + decode(dn, d, n, rows))

            @pl.when(z == nz - 1)
            def _():
                encode(send, d, n, part[...])

            c_dn(d, n).start()

        return carry

    lax.fori_loop(0, sends, step, 0)

    a_complete(nz - 1)

    def finish(n, carry):
        o_ref[:, columns(n)] += jnp.dot(a_all[z], b_all[n], preferred_element_type=jnp.float32)

        @pl.when(z > 0)
        def _():
            c_up(z, n).wait_recv()
            o_ref[:, columns(n)] += decode(up, z, n, rows)

        @pl.when(z < nz - 1)
        def _():
            c_dn(z, n).wait_recv()
            o_ref[:, columns(n)] += decode(dn, z, n, rows)

        return carry

    lax.fori_loop(0, nc, finish, 0)

    def drain_a(i, carry):
        a_y(i).wait_send()
        for j in range(2):
            a_x(i, j).wait_send()
        for j in range(4):
            a_c(i, j).wait_send()
        return carry

    def drain_b(n, carry):
        b_y(n).wait_send()
        return carry

    def drain_c(t, carry):
        d, n = t // nc, t % nc

        @pl.when(d != z)
        def _():
            c_up(d, n).wait_send()

        return carry

    lax.fori_loop(0, nz, drain_a, 0)
    lax.fori_loop(0, nc, drain_b, 0)
    lax.fori_loop(0, nz * nc, drain_c, 0)


def ladder_kernel(amplitudes, integrals, old_residual):
    nz, nc = lax.axis_size("wide") // 2, CHUNKS
    rows, cols = old_residual.shape
    depth = 2 * integrals.shape[0]
    tile = cols // nc
    dma = pltpu.SemaphoreType.DMA
    return pl.pallas_call(
        functools.partial(kernel, nz, nc),
        out_shape=jax.ShapeDtypeStruct((rows, cols), jnp.float32),
        in_specs=[pl.BlockSpec(memory_space=pl.ANY)] * 3,
        out_specs=pl.BlockSpec(memory_space=pltpu.VMEM),
        scratch_shapes=[
            pltpu.VMEM((nz, rows, depth), jnp.bfloat16),
            pltpu.VMEM((nc, depth, tile), jnp.bfloat16),
            pltpu.VMEM((rows, tile), jnp.float32),
            pltpu.VMEM((nz, nc, rows + SCALE_ROWS, tile), jnp.bfloat16),
            pltpu.VMEM((nz, nc, rows + SCALE_ROWS, tile), jnp.bfloat16),
            pltpu.VMEM((nz, nc, rows + SCALE_ROWS, tile), jnp.bfloat16),
            dma, dma((nz,)), dma((nc,)),
            dma((nz,)), dma((nz,)),
            dma((nz, 2)), dma((nz, 2)),
            dma((nz, 4)), dma((nz, 4)),
            dma((nc,)), dma((nc,)),
            dma((nz, nc)), dma((nz, nc)), dma((nz, nc)),
        ],
        compiler_params=pltpu.CompilerParams(
            collective_id=0, has_side_effects=True, vmem_limit_bytes=50 * 1024 * 1024),
        cost_estimate=pl.CostEstimate(
            flops=2 * nz * rows * depth * cols, bytes_accessed=8 * rows * cols, transcendentals=0),
    )(amplitudes, integrals, old_residual)


def broadcast(value, axis, source):
    kept = jnp.where(lax.axis_index(axis) == source, value, 0).astype(value.dtype)
    return lax.psum(kept, axis)


def ladder_gathered(amplitudes, integrals, old_residual):
    panels = lax.axis_size("narrow")
    sub_rows = integrals.shape[0] // panels
    stacked = integrals.reshape(panels, sub_rows, integrals.shape[1])
    total = old_residual
    row_amps = lax.all_to_all(amplitudes, "wide", split_axis=0, concat_axis=1, tiled=True)
    for column in range(panels):
        panel = broadcast(row_amps, "narrow", column)
        panel_ints = lax.all_gather(stacked[column], "wide", axis=0, tiled=True)
        total = total + jnp.dot(panel, panel_ints, preferred_element_type=jnp.float32)
    return total


def per_device(amplitudes, integrals, old_residual):
    if amplitudes.shape[1] % 128 or lax.axis_size("narrow") != 4 or lax.axis_size("wide") > 8:
        return ladder_gathered(amplitudes, integrals, old_residual)
    return ladder_kernel(amplitudes, integrals, old_residual)


def solution(mesh):
    placed = (P(None, ("wide", "narrow")), P("wide", "narrow"), P("wide", "narrow"))
    return jax.shard_map(
        per_device, mesh=mesh, in_specs=placed, out_specs=P("wide", "narrow"), check_vma=False
    )
```

```python
import functools

import jax
import jax.numpy as jnp
from jax import lax
from jax.experimental import pallas as pl
from jax.experimental.pallas import tpu as pltpu
from jax.sharding import PartitionSpec as P

SCALE_ROWS = 16
KEEP = 46000.0
CHUNKS = 8
AHEAD = 6
MESH = pl.DeviceIdType.MESH


def encode(ref, d, n, value):
    rows = value.shape[0]
    peak = jnp.max(jnp.abs(value), axis=0, keepdims=True)
    scale = (peak * 1.01 + 1e-30).astype(jnp.bfloat16)
    q = value * (KEEP / scale.astype(jnp.float32))
    q2 = q * q
    q4 = q2 * q2
    ref[d, n, :rows] = (q4 * q2 * (q * jnp.abs(q))).astype(jnp.bfloat16)
    ref[d, n, rows:] = jnp.broadcast_to(scale, (SCALE_ROWS, value.shape[1]))


def decode(ref, d, n, rows):
    code = ref[d, n, :rows].astype(jnp.float32)
    scale = ref[d, n, rows:].astype(jnp.float32)[:1]
    r1 = lax.rsqrt(jnp.maximum(jnp.abs(code), 1.2e-38))
    r2 = lax.rsqrt(r1)
    root = r2 * lax.rsqrt(r2)
    return jnp.where(code < 0, -root, root) * (scale * (1.0 / KEEP))


def kernel(nz, nc, a_ref, b_ref, r_ref, o_ref, a_all, b_all, part, send, up, dn,
           r_s, al_s, bl_s, ay_s, ay_r, ax_s, ax_r, ac_s, ac_r, by_s, by_r, z_s, up_r, dn_r):
    w, m = lax.axis_index("wide"), lax.axis_index("narrow")
    z, y, x, c = w // 2, w % 2, m // 2, m % 2
    rows, cols = r_ref.shape
    ka, kb = a_ref.shape[1], b_ref.shape[0]
    tile = cols // nc
    to_y = (z * 2 + 1 - y, m)
    to_x = (w, (1 - x) * 2 + c)
    to_c = (w, x * 2 + 1 - c)
    above, below = (w + 2, m), (w - 2, m)
    high = (2 * z) // nz

    own = z + (1 - high) * (nz - 1 - 2 * z)

    def order(i):
        last = (i + 1) // nz
        k = last * own + (1 - last) * (i + (i + nz - own) // nz)
        return k + (1 - high) * (nz - 1 - 2 * k)

    def piece(yy, xx, cc):
        return pl.ds(pl.multiple_of((yy * 4 + xx * 2 + cc) * ka, ka), ka)

    def rows_of(d, yy):
        return a_ref.at[pl.ds(pl.multiple_of((d * 2 + yy) * rows, rows), rows), :]

    def columns(n):
        return pl.ds(pl.multiple_of(n * tile, tile), tile)

    def remote(src, dst, s, r, to):
        return pltpu.make_async_remote_copy(
            src_ref=src, dst_ref=dst, send_sem=s, recv_sem=r, device_id=to, device_id_type=MESH)

    def a_local(i):
        d = order(i)
        return pltpu.make_async_copy(rows_of(d, y), a_all.at[d, :, piece(y, x, c)], al_s.at[i])

    def b_local(n):
        return pltpu.make_async_copy(
            b_ref.at[:, columns(n)], b_all.at[n, pl.ds(pl.multiple_of(y * kb, kb), kb)], bl_s.at[n])

    def a_y(i):
        d = order(i)
        return remote(rows_of(d, 1 - y), a_all.at[d, :, piece(y, x, c)], ay_s.at[i], ay_r.at[i], to_y)

    def a_x(i, j):
        d = order(i)
        src = rows_of(d, y) if j == 0 else a_all.at[d, :, piece(1 - y, x, c)]
        dst = a_all.at[d, :, piece(y if j == 0 else 1 - y, x, c)]
        return remote(src, dst, ax_s.at[i, j], ax_r.at[i, j], to_x)

    def a_c(i, j):
        d = order(i)
        here = piece(y if j % 2 == 0 else 1 - y, x if j < 2 else 1 - x, c)
        src = rows_of(d, y) if j == 0 else a_all.at[d, :, here]
        return remote(src, a_all.at[d, :, here], ac_s.at[i, j], ac_r.at[i, j], to_c)

    def b_y(n):
        return remote(b_ref.at[:, columns(n)], b_all.at[n, pl.ds(pl.multiple_of(y * kb, kb), kb)],
                      by_s.at[n], by_r.at[n], to_y)

    def c_up(d, n):
        return remote(send.at[d, n], up.at[d, n], z_s.at[d, n], up_r.at[d, n], above)

    def c_dn(d, n):
        return remote(send.at[d, n], dn.at[d, n], z_s.at[d, n], dn_r.at[d, n], below)

    residual = pltpu.make_async_copy(r_ref, o_ref, r_s)
    for i in range(nz):
        a_local(i).start()
    for n in range(nc):
        b_local(n).start()
    residual.start()

    barrier = pltpu.get_barrier_semaphore()
    for to in (to_y, to_x, to_c):
        pl.semaphore_signal(barrier, inc=1, device_id=to, device_id_type=MESH)

    @pl.when(z > 0)
    def _():
        pl.semaphore_signal(barrier, inc=1, device_id=below, device_id_type=MESH)

    @pl.when(z < nz - 1)
    def _():
        pl.semaphore_signal(barrier, inc=1, device_id=above, device_id_type=MESH)

    pl.semaphore_wait(barrier, 3 + (z + nz - 1) // nz + (2 * nz - 2 - z) // nz)

    queue = []
    for e in range(nz - 1):
        queue += [("a", e), ("b", e)]
    queue += [("b", n) for n in range(nz - 1, nc)] + [("a", nz - 1)]

    def start_y(k):
        if k < len(queue):
            (a_y if queue[k][0] == "a" else b_y)(queue[k][1]).start()

    def start_own(i):
        if i < nz:
            a_x(i, 0).start()
            a_c(i, 0).start()

    def a_arrives(i):
        a_y(i).wait_recv()
        start_y(queue.index(("a", i)) + AHEAD)
        a_x(i, 1).start()
        a_c(i, 1).start()
        start_own(i + 2)

    def b_arrives(n):
        b_local(n).wait()
        b_y(n).wait_recv()
        start_y(queue.index(("b", n)) + AHEAD)

    def a_complete(i):
        a_x(i, 0).wait_recv()
        a_c(i, 2).start()
        a_x(i, 1).wait_recv()
        a_c(i, 3).start()
        a_local(i).wait()
        for j in range(4):
            a_c(i, j).wait_recv()

    for k in range(AHEAD):
        start_y(k)
    start_own(0)
    start_own(1)
    residual.wait()

    head = [(0, 0)]
    for e in range(1, nz - 1):
        head += [(i, e) for i in range(e)] + [(e, n) for n in range(e + 1)]
    sends = (nz - 1) * nc

    def step(t, carry):
        i = (t - len(head)) % (nz - 1)
        n = nz - 1 + (t - len(head)) // (nz - 1)
        for k, (head_i, head_n) in enumerate(head):
            i = jnp.where(t == k, head_i, i)
            n = jnp.where(t == k, head_n, n)
        d = order(i)

        @pl.when(t == 0)
        def _():
            a_arrives(0)
            b_arrives(0)
            a_complete(0)

        for e in range(1, nz - 1):
            @pl.when(t == head.index((0, e)))
            def _():
                a_arrives(e)
                b_arrives(e)

            @pl.when(t == head.index((e, 0)))
            def _():
                a_complete(e)

        for e in range(nz - 1, nc):
            @pl.when(t == len(head) + (e - nz + 1) * (nz - 1))
            def _():
                b_arrives(e)

        part[...] = jnp.dot(a_all[d], b_all[n], preferred_element_type=jnp.float32)

        @pl.when(d > z)
        def _():
            @pl.when(z > 0)
            def _():
                c_up(d, n).wait_recv()
                encode(send, d, n, part[...] + decode(up, d, n, rows))

            @pl.when(z == 0)
            def _():
                encode(send, d, n, part[...])

            c_up(d, n).start()

        @pl.when(d < z)
        def _():
            @pl.when(z < nz - 1)
            def _():
                c_dn(d, n).wait_recv()
                encode(send, d, n, part[...] + decode(dn, d, n, rows))

            @pl.when(z == nz - 1)
            def _():
                encode(send, d, n, part[...])

            c_dn(d, n).start()

        return carry

    lax.fori_loop(0, sends, step, 0)

    a_arrives(nz - 1)
    a_complete(nz - 1)

    def finish(n, carry):
        o_ref[:, columns(n)] += jnp.dot(a_all[z], b_all[n], preferred_element_type=jnp.float32)

        @pl.when(z > 0)
        def _():
            c_up(z, n).wait_recv()
            o_ref[:, columns(n)] += decode(up, z, n, rows)

        @pl.when(z < nz - 1)
        def _():
            c_dn(z, n).wait_recv()
            o_ref[:, columns(n)] += decode(dn, z, n, rows)

        return carry

    lax.fori_loop(0, nc, finish, 0)

    def drain_a(i, carry):
        a_y(i).wait_send()
        for j in range(2):
            a_x(i, j).wait_send()
        for j in range(4):
            a_c(i, j).wait_send()
        return carry

    def drain_b(n, carry):
        b_y(n).wait_send()
        return carry

    def drain_c(t, carry):
        d, n = t // nc, t % nc

        @pl.when(d != z)
        def _():
            c_up(d, n).wait_send()

        return carry

    lax.fori_loop(0, nz, drain_a, 0)
    lax.fori_loop(0, nc, drain_b, 0)
    lax.fori_loop(0, nz * nc, drain_c, 0)


def ladder_kernel(amplitudes, integrals, old_residual):
    nz, nc = lax.axis_size("wide") // 2, CHUNKS
    rows, cols = old_residual.shape
    depth = 2 * integrals.shape[0]
    tile = cols // nc
    dma = pltpu.SemaphoreType.DMA
    return pl.pallas_call(
        functools.partial(kernel, nz, nc),
        out_shape=jax.ShapeDtypeStruct((rows, cols), jnp.float32),
        in_specs=[pl.BlockSpec(memory_space=pl.ANY)] * 3,
        out_specs=pl.BlockSpec(memory_space=pltpu.VMEM),
        scratch_shapes=[
            pltpu.VMEM((nz, rows, depth), jnp.bfloat16),
            pltpu.VMEM((nc, depth, tile), jnp.bfloat16),
            pltpu.VMEM((rows, tile), jnp.float32),
            pltpu.VMEM((nz, nc, rows + SCALE_ROWS, tile), jnp.bfloat16),
            pltpu.VMEM((nz, nc, rows + SCALE_ROWS, tile), jnp.bfloat16),
            pltpu.VMEM((nz, nc, rows + SCALE_ROWS, tile), jnp.bfloat16),
            dma, dma((nz,)), dma((nc,)),
            dma((nz,)), dma((nz,)),
            dma((nz, 2)), dma((nz, 2)),
            dma((nz, 4)), dma((nz, 4)),
            dma((nc,)), dma((nc,)),
            dma((nz, nc)), dma((nz, nc)), dma((nz, nc)),
        ],
        compiler_params=pltpu.CompilerParams(
            collective_id=0, has_side_effects=True, vmem_limit_bytes=62 * 1024 * 1024),
        cost_estimate=pl.CostEstimate(
            flops=2 * nz * rows * depth * cols, bytes_accessed=8 * rows * cols, transcendentals=0),
    )(amplitudes, integrals, old_residual)


def broadcast(value, axis, source):
    kept = jnp.where(lax.axis_index(axis) == source, value, 0).astype(value.dtype)
    return lax.psum(kept, axis)


def ladder_gathered(amplitudes, integrals, old_residual):
    panels = lax.axis_size("narrow")
    sub_rows = integrals.shape[0] // panels
    stacked = integrals.reshape(panels, sub_rows, integrals.shape[1])
    total = old_residual
    row_amps = lax.all_to_all(amplitudes, "wide", split_axis=0, concat_axis=1, tiled=True)
    for column in range(panels):
        panel = broadcast(row_amps, "narrow", column)
        panel_ints = lax.all_gather(stacked[column], "wide", axis=0, tiled=True)
        total = total + jnp.dot(panel, panel_ints, preferred_element_type=jnp.float32)
    return total


def per_device(amplitudes, integrals, old_residual):
    if amplitudes.shape[1] % 128 or lax.axis_size("narrow") != 4 or lax.axis_size("wide") > 8:
        return ladder_gathered(amplitudes, integrals, old_residual)
    return ladder_kernel(amplitudes, integrals, old_residual)


def solution(mesh):
    placed = (P(None, ("wide", "narrow")), P("wide", "narrow"), P("wide", "narrow"))
    return jax.shard_map(
        per_device, mesh=mesh, in_specs=placed, out_specs=P("wide", "narrow"), check_vma=False
    )
```

```python
import functools

import jax
import jax.numpy as jnp
from jax import lax
from jax.experimental import pallas as pl
from jax.experimental.pallas import tpu as pltpu
from jax.sharding import PartitionSpec as P

SCALE_ROWS = 16
KEEP = 46000.0
CHUNKS = 8
AHEAD = 2
MESH = pl.DeviceIdType.MESH


def encode(ref, d, n, value):
    rows = value.shape[0]
    peak = jnp.max(jnp.abs(value), axis=0, keepdims=True)
    scale = (peak * 1.01 + 1e-30).astype(jnp.bfloat16)
    q = value * (KEEP / scale.astype(jnp.float32))
    q2 = q * q
    q4 = q2 * q2
    ref[d, n, :rows] = (q4 * q2 * (q * jnp.abs(q))).astype(jnp.bfloat16)
    ref[d, n, rows:] = jnp.broadcast_to(scale, (SCALE_ROWS, value.shape[1]))


def decode(ref, d, n, rows):
    code = ref[d, n, :rows].astype(jnp.float32)
    scale = ref[d, n, rows:].astype(jnp.float32)[:1]
    r1 = lax.rsqrt(jnp.maximum(jnp.abs(code), 1.2e-38))
    r2 = lax.rsqrt(r1)
    root = r2 * lax.rsqrt(r2)
    return jnp.where(code < 0, -root, root) * (scale * (1.0 / KEEP))


def kernel(nz, nc, a_ref, b_ref, r_ref, o_ref, a_all, b_all, part, send, up, dn,
           r_s, al_s, bl_s, ay_s, ay_r, ax_s, ax_r, ac_s, ac_r, by_s, by_r, z_s, up_r, dn_r):
    w, m = lax.axis_index("wide"), lax.axis_index("narrow")
    z, y, x, c = w // 2, w % 2, m // 2, m % 2
    rows, cols = r_ref.shape
    ka, kb = a_ref.shape[1], b_ref.shape[0]
    tile = cols // nc
    to_y = (z * 2 + 1 - y, m)
    to_x = (w, (1 - x) * 2 + c)
    to_c = (w, x * 2 + 1 - c)
    above, below = (w + 2, m), (w - 2, m)
    high = (2 * z) // nz

    own = z + (1 - high) * (nz - 1 - 2 * z)

    def order(i):
        last = (i + 1) // nz
        k = last * own + (1 - last) * (i + (i + nz - own) // nz)
        return k + (1 - high) * (nz - 1 - 2 * k)

    def piece(yy, xx, cc):
        return yy * 4 + xx * 2 + cc

    def rows_of(d, yy):
        return a_ref.at[pl.ds(pl.multiple_of((d * 2 + yy) * rows, rows), rows), :]

    def columns(n):
        return pl.ds(pl.multiple_of(n * tile, tile), tile)

    def remote(src, dst, s, r, to):
        return pltpu.make_async_remote_copy(
            src_ref=src, dst_ref=dst, send_sem=s, recv_sem=r, device_id=to, device_id_type=MESH)

    def a_local(i):
        d = order(i)
        return pltpu.make_async_copy(rows_of(d, y), a_all.at[d, piece(y, x, c)], al_s.at[i])

    def b_local(n):
        return pltpu.make_async_copy(
            b_ref.at[:, columns(n)], b_all.at[n, pl.ds(pl.multiple_of(y * kb, kb), kb)], bl_s.at[n])

    def a_y(i):
        d = order(i)
        return remote(rows_of(d, 1 - y), a_all.at[d, piece(y, x, c)], ay_s.at[i], ay_r.at[i], to_y)

    def a_x(i, j):
        d = order(i)
        src = rows_of(d, y) if j == 0 else a_all.at[d, piece(1 - y, x, c)]
        dst = a_all.at[d, piece(y if j == 0 else 1 - y, x, c)]
        return remote(src, dst, ax_s.at[i, j], ax_r.at[i, j], to_x)

    def a_c(i, j):
        d = order(i)
        here = piece(y if j % 2 == 0 else 1 - y, x if j < 2 else 1 - x, c)
        src = rows_of(d, y) if j == 0 else a_all.at[d, here]
        return remote(src, a_all.at[d, here], ac_s.at[i, j], ac_r.at[i, j], to_c)

    def b_y(n):
        half = b_all.at[n, pl.ds(pl.multiple_of(y * kb, kb), kb)]
        return remote(half, half, by_s.at[n], by_r.at[n], to_y)

    def c_up(d, n):
        return remote(send.at[d, n], up.at[d, n], z_s.at[d, n], up_r.at[d, n], above)

    def c_dn(d, n):
        return remote(send.at[d, n], dn.at[d, n], z_s.at[d, n], dn_r.at[d, n], below)

    residual = pltpu.make_async_copy(r_ref, o_ref, r_s)
    def product(d, n):
        left = jnp.concatenate([a_all[d, p] for p in range(8)], axis=1)
        return jnp.dot(left, b_all[n], preferred_element_type=jnp.float32)

    for n in range(nc):
        b_local(n).start()
    for i in range(nz):
        a_local(i).start()
    residual.start()

    barrier = pltpu.get_barrier_semaphore()
    for to in (to_y, to_x, to_c):
        pl.semaphore_signal(barrier, inc=1, device_id=to, device_id_type=MESH)

    @pl.when(z > 0)
    def _():
        pl.semaphore_signal(barrier, inc=1, device_id=below, device_id_type=MESH)

    @pl.when(z < nz - 1)
    def _():
        pl.semaphore_signal(barrier, inc=1, device_id=above, device_id_type=MESH)

    pl.semaphore_wait(barrier, 3 + (z + nz - 1) // nz + (2 * nz - 2 - z) // nz)

    queue = []
    for e in range(nz - 1):
        queue += [("a", e), ("b", e)]
    queue += [("b", n) for n in range(nz - 1, nc)] + [("a", nz - 1)]

    def start_y(k):
        if k < len(queue):
            kind, e = queue[k]
            if kind == "b":
                b_local(e).wait()
            (a_y if kind == "a" else b_y)(e).start()

    def start_own(i):
        if i < nz:
            a_x(i, 0).start()
            a_c(i, 0).start()

    def a_arrives(i):
        a_y(i).wait_recv()
        start_y(queue.index(("a", i)) + AHEAD)
        a_x(i, 1).start()
        a_c(i, 1).start()
        start_own(i + 2)

    def b_arrives(n):
        b_y(n).wait_recv()
        start_y(queue.index(("b", n)) + AHEAD)

    def a_complete(i):
        a_x(i, 0).wait_recv()
        a_c(i, 2).start()
        a_x(i, 1).wait_recv()
        a_c(i, 3).start()
        a_local(i).wait()
        for j in range(4):
            a_c(i, j).wait_recv()

    for k in range(AHEAD):
        start_y(k)
    start_own(0)
    start_own(1)
    residual.wait()

    head = [(0, 0)]
    for e in range(1, nz - 1):
        head += [(i, e) for i in range(e)] + [(e, n) for n in range(e + 1)]
    sends = (nz - 1) * nc

    def step(t, carry):
        i = (t - len(head)) % (nz - 1)
        n = nz - 1 + (t - len(head)) // (nz - 1)
        for k, (head_i, head_n) in enumerate(head):
            i = jnp.where(t == k, head_i, i)
            n = jnp.where(t == k, head_n, n)
        d = order(i)

        @pl.when(t == 0)
        def _():
            a_arrives(0)
            b_arrives(0)
            a_complete(0)

        for e in range(1, nz - 1):
            @pl.when(t == head.index((0, e)))
            def _():
                a_arrives(e)
                b_arrives(e)

            @pl.when(t == head.index((e, 0)))
            def _():
                a_complete(e)

        for e in range(nz - 1, nc):
            @pl.when(t == len(head) + (e - nz + 1) * (nz - 1))
            def _():
                b_arrives(e)

        part[...] = product(d, n)

        @pl.when(d > z)
        def _():
            @pl.when(z > 0)
            def _():
                c_up(d, n).wait_recv()
                encode(send, d, n, part[...] + decode(up, d, n, rows))

            @pl.when(z == 0)
            def _():
                encode(send, d, n, part[...])

            c_up(d, n).start()

        @pl.when(d < z)
        def _():
            @pl.when(z < nz - 1)
            def _():
                c_dn(d, n).wait_recv()
                encode(send, d, n, part[...] + decode(dn, d, n, rows))

            @pl.when(z == nz - 1)
            def _():
                encode(send, d, n, part[...])

            c_dn(d, n).start()

        return carry

    lax.fori_loop(0, sends, step, 0)

    a_arrives(nz - 1)
    a_complete(nz - 1)

    def finish(n, carry):
        o_ref[:, columns(n)] += product(z, n)

        @pl.when(z > 0)
        def _():
            c_up(z, n).wait_recv()
            o_ref[:, columns(n)] += decode(up, z, n, rows)

        @pl.when(z < nz - 1)
        def _():
            c_dn(z, n).wait_recv()
            o_ref[:, columns(n)] += decode(dn, z, n, rows)

        return carry

    lax.fori_loop(0, nc, finish, 0)

    def drain_a(i, carry):
        a_y(i).wait_send()
        for j in range(2):
            a_x(i, j).wait_send()
        for j in range(4):
            a_c(i, j).wait_send()
        return carry

    def drain_b(n, carry):
        b_y(n).wait_send()
        return carry

    def drain_c(t, carry):
        d, n = t // nc, t % nc

        @pl.when(d != z)
        def _():
            c_up(d, n).wait_send()

        return carry

    lax.fori_loop(0, nz, drain_a, 0)
    lax.fori_loop(0, nc, drain_b, 0)
    lax.fori_loop(0, nz * nc, drain_c, 0)


def ladder_kernel(amplitudes, integrals, old_residual):
    nz, nc = lax.axis_size("wide") // 2, CHUNKS
    rows, cols = old_residual.shape
    depth = 2 * integrals.shape[0]
    tile = cols // nc
    dma = pltpu.SemaphoreType.DMA
    return pl.pallas_call(
        functools.partial(kernel, nz, nc),
        out_shape=jax.ShapeDtypeStruct((rows, cols), jnp.float32),
        in_specs=[pl.BlockSpec(memory_space=pl.ANY)] * 3,
        out_specs=pl.BlockSpec(memory_space=pltpu.VMEM),
        scratch_shapes=[
            pltpu.VMEM((nz, 8, rows, amplitudes.shape[1]), jnp.bfloat16),
            pltpu.VMEM((nc, depth, tile), jnp.bfloat16),
            pltpu.VMEM((rows, tile), jnp.float32),
            pltpu.VMEM((nz, nc, rows + SCALE_ROWS, tile), jnp.bfloat16),
            pltpu.VMEM((nz, nc, rows + SCALE_ROWS, tile), jnp.bfloat16),
            pltpu.VMEM((nz, nc, rows + SCALE_ROWS, tile), jnp.bfloat16),
            dma, dma((nz,)), dma((nc,)),
            dma((nz,)), dma((nz,)),
            dma((nz, 2)), dma((nz, 2)),
            dma((nz, 4)), dma((nz, 4)),
            dma((nc,)), dma((nc,)),
            dma((nz, nc)), dma((nz, nc)), dma((nz, nc)),
        ],
        compiler_params=pltpu.CompilerParams(
            collective_id=0, has_side_effects=True, vmem_limit_bytes=62 * 1024 * 1024),
        cost_estimate=pl.CostEstimate(
            flops=2 * nz * rows * depth * cols, bytes_accessed=8 * rows * cols, transcendentals=0),
    )(amplitudes, integrals, old_residual)


def broadcast(value, axis, source):
    kept = jnp.where(lax.axis_index(axis) == source, value, 0).astype(value.dtype)
    return lax.psum(kept, axis)


def ladder_gathered(amplitudes, integrals, old_residual):
    panels = lax.axis_size("narrow")
    sub_rows = integrals.shape[0] // panels
    stacked = integrals.reshape(panels, sub_rows, integrals.shape[1])
    total = old_residual
    row_amps = lax.all_to_all(amplitudes, "wide", split_axis=0, concat_axis=1, tiled=True)
    for column in range(panels):
        panel = broadcast(row_amps, "narrow", column)
        panel_ints = lax.all_gather(stacked[column], "wide", axis=0, tiled=True)
        total = total + jnp.dot(panel, panel_ints, preferred_element_type=jnp.float32)
    return total


def per_device(amplitudes, integrals, old_residual):
    if amplitudes.shape[1] % 128 or lax.axis_size("narrow") != 4 or lax.axis_size("wide") > 8:
        return ladder_gathered(amplitudes, integrals, old_residual)
    return ladder_kernel(amplitudes, integrals, old_residual)


def solution(mesh):
    placed = (P(None, ("wide", "narrow")), P("wide", "narrow"), P("wide", "narrow"))
    return jax.shard_map(
        per_device, mesh=mesh, in_specs=placed, out_specs=P("wide", "narrow"), check_vma=False
    )
```

```python
import functools

import jax
import jax.numpy as jnp
from jax import lax
from jax.experimental import pallas as pl
from jax.experimental.pallas import tpu as pltpu
from jax.sharding import PartitionSpec as P

SCALE_ROWS = 16
KEEP = 46000.0
CHUNKS = 8
AHEAD = 3
MESH = pl.DeviceIdType.MESH


def encode(ref, d, n, value):
    rows = value.shape[0]
    peak = jnp.max(jnp.abs(value), axis=0, keepdims=True)
    scale = (peak * 1.01 + 1e-30).astype(jnp.bfloat16)
    q = value * (KEEP / scale.astype(jnp.float32))
    q2 = q * q
    q4 = q2 * q2
    ref[d, n, :rows] = (q4 * q2 * (q * jnp.abs(q))).astype(jnp.bfloat16)
    ref[d, n, rows:] = jnp.broadcast_to(scale, (SCALE_ROWS, value.shape[1]))


def decode(ref, d, n, rows):
    code = ref[d, n, :rows].astype(jnp.float32)
    scale = ref[d, n, rows:].astype(jnp.float32)[:1]
    r1 = lax.rsqrt(jnp.maximum(jnp.abs(code), 1.2e-38))
    r2 = lax.rsqrt(r1)
    root = r2 * lax.rsqrt(r2)
    return jnp.where(code < 0, -root, root) * (scale * (1.0 / KEEP))


def kernel(nz, nc, a_ref, b_ref, r_ref, o_ref, a_all, b_all, part, send, up, dn,
           r_s, al_s, bl_s, ay_s, ay_r, ax_s, ax_r, ac_s, ac_r, by_s, by_r, z_s, up_r, dn_r):
    w, m = lax.axis_index("wide"), lax.axis_index("narrow")
    z, y, x, c = w // 2, w % 2, m // 2, m % 2
    rows, cols = r_ref.shape
    ka, kb = a_ref.shape[1], b_ref.shape[0]
    tile = cols // nc
    to_y = (z * 2 + 1 - y, m)
    to_x = (w, (1 - x) * 2 + c)
    to_c = (w, x * 2 + 1 - c)
    above, below = (w + 2, m), (w - 2, m)
    high = (2 * z) // nz

    own = z + (1 - high) * (nz - 1 - 2 * z)

    def order(i):
        last = (i + 1) // nz
        k = last * own + (1 - last) * (i + (i + nz - own) // nz)
        return k + (1 - high) * (nz - 1 - 2 * k)

    def piece(yy, xx, cc):
        return yy * 4 + xx * 2 + cc

    def rows_of(d, yy):
        return a_ref.at[pl.ds(pl.multiple_of((d * 2 + yy) * rows, rows), rows), :]

    def columns(n):
        return pl.ds(pl.multiple_of(n * tile, tile), tile)

    def remote(src, dst, s, r, to):
        return pltpu.make_async_remote_copy(
            src_ref=src, dst_ref=dst, send_sem=s, recv_sem=r, device_id=to, device_id_type=MESH)

    def a_local(i):
        d = order(i)
        return pltpu.make_async_copy(rows_of(d, y), a_all.at[d, piece(y, x, c)], al_s.at[i])

    def b_local(n):
        return pltpu.make_async_copy(
            b_ref.at[:, columns(n)], b_all.at[n, pl.ds(pl.multiple_of(y * kb, kb), kb)], bl_s.at[n])

    def a_y(i):
        d = order(i)
        return remote(rows_of(d, 1 - y), a_all.at[d, piece(y, x, c)], ay_s.at[i], ay_r.at[i], to_y)

    def a_x(i, j):
        d = order(i)
        src = rows_of(d, y) if j == 0 else a_all.at[d, piece(1 - y, x, c)]
        dst = a_all.at[d, piece(y if j == 0 else 1 - y, x, c)]
        return remote(src, dst, ax_s.at[i, j], ax_r.at[i, j], to_x)

    def a_c(i, j):
        d = order(i)
        here = piece(y if j % 2 == 0 else 1 - y, x if j < 2 else 1 - x, c)
        src = rows_of(d, y) if j == 0 else a_all.at[d, here]
        return remote(src, a_all.at[d, here], ac_s.at[i, j], ac_r.at[i, j], to_c)

    def b_y(n):
        half = b_all.at[n, pl.ds(pl.multiple_of(y * kb, kb), kb)]
        return remote(half, half, by_s.at[n], by_r.at[n], to_y)

    def c_up(d, n):
        return remote(send.at[d, n], up.at[d, n], z_s.at[d, n], up_r.at[d, n], above)

    def c_dn(d, n):
        return remote(send.at[d, n], dn.at[d, n], z_s.at[d, n], dn_r.at[d, n], below)

    residual = pltpu.make_async_copy(r_ref, o_ref, r_s)
    def product(d, n):
        left = jnp.concatenate([a_all[d, p] for p in range(8)], axis=1)
        return jnp.dot(left, b_all[n], preferred_element_type=jnp.float32)

    for n in range(nc):
        b_local(n).start()
    for i in range(nz):
        a_local(i).start()
    residual.start()

    barrier = pltpu.get_barrier_semaphore()
    for to in (to_y, to_x, to_c):
        pl.semaphore_signal(barrier, inc=1, device_id=to, device_id_type=MESH)

    @pl.when(z > 0)
    def _():
        pl.semaphore_signal(barrier, inc=1, device_id=below, device_id_type=MESH)

    @pl.when(z < nz - 1)
    def _():
        pl.semaphore_signal(barrier, inc=1, device_id=above, device_id_type=MESH)

    pl.semaphore_wait(barrier, 3 + (z + nz - 1) // nz + (2 * nz - 2 - z) // nz)

    queue = []
    for e in range(nz - 1):
        queue += [("a", e), ("b", e)]
    queue += [("b", n) for n in range(nz - 1, nc - 2)] + [("a", nz - 1), ("b", nc - 2), ("b", nc - 1)]

    def start_y(k):
        if k < len(queue):
            kind, e = queue[k]
            if kind == "b":
                b_local(e).wait()
            (a_y if kind == "a" else b_y)(e).start()

    def start_own(i):
        if i < nz:
            a_x(i, 0).start()
            a_c(i, 0).start()

    def a_arrives(i):
        a_y(i).wait_recv()
        start_y(queue.index(("a", i)) + AHEAD)
        a_x(i, 1).start()
        a_c(i, 1).start()
        start_own(i + 2)

    def b_arrives(n):
        b_y(n).wait_recv()
        start_y(queue.index(("b", n)) + AHEAD)

    def a_complete(i):
        a_x(i, 0).wait_recv()
        a_c(i, 2).start()
        a_x(i, 1).wait_recv()
        a_c(i, 3).start()
        a_local(i).wait()
        for j in range(4):
            a_c(i, j).wait_recv()

    for k in range(AHEAD):
        start_y(k)
    start_own(0)
    start_own(1)
    residual.wait()

    head = [(0, 0)]
    for e in range(1, nz - 1):
        head += [(i, e) for i in range(e)] + [(e, n) for n in range(e + 1)]
    sends = (nz - 1) * nc

    def own_product(n, carry):
        o_ref[:, columns(n)] += product(z, n)
        return carry

    def add_arrivals(n, carry):
        @pl.when(z > 0)
        def _():
            c_up(z, n).wait_recv()
            o_ref[:, columns(n)] += decode(up, z, n, rows)

        @pl.when(z < nz - 1)
        def _():
            c_dn(z, n).wait_recv()
            o_ref[:, columns(n)] += decode(dn, z, n, rows)

        return carry

    def step(t, carry):
        i = (t - len(head)) % (nz - 1)
        n = nz - 1 + (t - len(head)) // (nz - 1)
        for k, (head_i, head_n) in enumerate(head):
            i = jnp.where(t == k, head_i, i)
            n = jnp.where(t == k, head_n, n)
        d = order(i)

        @pl.when(t == 0)
        def _():
            a_arrives(0)
            b_arrives(0)
            a_complete(0)

        for e in range(1, nz - 1):
            @pl.when(t == head.index((0, e)))
            def _():
                a_arrives(e)
                b_arrives(e)

            @pl.when(t == head.index((e, 0)))
            def _():
                a_complete(e)

        for e in range(nz - 1, nc):
            @pl.when(t == len(head) + (e - nz + 1) * (nz - 1))
            def _():
                if e == nc - 2:
                    a_arrives(nz - 1)
                if e == nc - 1:
                    a_complete(nz - 1)
                    lax.fori_loop(0, nc - 1, own_product, 0)
                    lax.fori_loop(0, nc - 4, add_arrivals, 0)
                b_arrives(e)

        part[...] = product(d, n)

        @pl.when(d > z)
        def _():
            @pl.when(z > 0)
            def _():
                c_up(d, n).wait_recv()
                encode(send, d, n, part[...] + decode(up, d, n, rows))

            @pl.when(z == 0)
            def _():
                encode(send, d, n, part[...])

            c_up(d, n).start()

        @pl.when(d < z)
        def _():
            @pl.when(z < nz - 1)
            def _():
                c_dn(d, n).wait_recv()
                encode(send, d, n, part[...] + decode(dn, d, n, rows))

            @pl.when(z == nz - 1)
            def _():
                encode(send, d, n, part[...])

            c_dn(d, n).start()

        return carry

    lax.fori_loop(0, sends, step, 0)

    own_product(nc - 1, 0)
    lax.fori_loop(nc - 4, nc, add_arrivals, 0)

    def drain_a(i, carry):
        a_y(i).wait_send()
        for j in range(2):
            a_x(i, j).wait_send()
        for j in range(4):
            a_c(i, j).wait_send()
        return carry

    def drain_b(n, carry):
        b_y(n).wait_send()
        return carry

    def drain_c(t, carry):
        d, n = t // nc, t % nc

        @pl.when(d != z)
        def _():
            c_up(d, n).wait_send()

        return carry

    lax.fori_loop(0, nz, drain_a, 0)
    lax.fori_loop(0, nc, drain_b, 0)
    lax.fori_loop(0, nz * nc, drain_c, 0)


def ladder_kernel(amplitudes, integrals, old_residual):
    nz, nc = lax.axis_size("wide") // 2, CHUNKS
    rows, cols = old_residual.shape
    depth = 2 * integrals.shape[0]
    tile = cols // nc
    dma = pltpu.SemaphoreType.DMA
    return pl.pallas_call(
        functools.partial(kernel, nz, nc),
        out_shape=jax.ShapeDtypeStruct((rows, cols), jnp.float32),
        in_specs=[pl.BlockSpec(memory_space=pl.ANY)] * 3,
        out_specs=pl.BlockSpec(memory_space=pltpu.VMEM),
        scratch_shapes=[
            pltpu.VMEM((nz, 8, rows, amplitudes.shape[1]), jnp.bfloat16),
            pltpu.VMEM((nc, depth, tile), jnp.bfloat16),
            pltpu.VMEM((rows, tile), jnp.float32),
            pltpu.VMEM((nz, nc, rows + SCALE_ROWS, tile), jnp.bfloat16),
            pltpu.VMEM((nz, nc, rows + SCALE_ROWS, tile), jnp.bfloat16),
            pltpu.VMEM((nz, nc, rows + SCALE_ROWS, tile), jnp.bfloat16),
            dma, dma((nz,)), dma((nc,)),
            dma((nz,)), dma((nz,)),
            dma((nz, 2)), dma((nz, 2)),
            dma((nz, 4)), dma((nz, 4)),
            dma((nc,)), dma((nc,)),
            dma((nz, nc)), dma((nz, nc)), dma((nz, nc)),
        ],
        compiler_params=pltpu.CompilerParams(
            collective_id=0, has_side_effects=True, vmem_limit_bytes=50 * 1024 * 1024),
        cost_estimate=pl.CostEstimate(
            flops=2 * nz * rows * depth * cols, bytes_accessed=8 * rows * cols, transcendentals=0),
    )(amplitudes, integrals, old_residual)


def broadcast(value, axis, source):
    kept = jnp.where(lax.axis_index(axis) == source, value, 0).astype(value.dtype)
    return lax.psum(kept, axis)


def ladder_gathered(amplitudes, integrals, old_residual):
    panels = lax.axis_size("narrow")
    sub_rows = integrals.shape[0] // panels
    stacked = integrals.reshape(panels, sub_rows, integrals.shape[1])
    total = old_residual
    row_amps = lax.all_to_all(amplitudes, "wide", split_axis=0, concat_axis=1, tiled=True)
    for column in range(panels):
        panel = broadcast(row_amps, "narrow", column)
        panel_ints = lax.all_gather(stacked[column], "wide", axis=0, tiled=True)
        total = total + jnp.dot(panel, panel_ints, preferred_element_type=jnp.float32)
    return total


def per_device(amplitudes, integrals, old_residual):
    if amplitudes.shape[1] % 128 or lax.axis_size("narrow") != 4 or lax.axis_size("wide") > 8:
        return ladder_gathered(amplitudes, integrals, old_residual)
    return ladder_kernel(amplitudes, integrals, old_residual)


def solution(mesh):
    placed = (P(None, ("wide", "narrow")), P("wide", "narrow"), P("wide", "narrow"))
    return jax.shard_map(
        per_device, mesh=mesh, in_specs=placed, out_specs=P("wide", "narrow"), check_vma=False
    )
```

```python
import functools

import jax
import jax.numpy as jnp
from jax import lax
from jax.experimental import pallas as pl
from jax.experimental.pallas import tpu as pltpu
from jax.sharding import PartitionSpec as P

SCALE_ROWS = 16
KEEP = 46000.0
CHUNKS = 8
AHEAD = 3
MESH = pl.DeviceIdType.MESH


def encode(ref, d, n, value):
    rows = value.shape[0]
    peak = jnp.max(jnp.abs(value), axis=0, keepdims=True)
    scale = (peak * 1.01 + 1e-30).astype(jnp.bfloat16)
    q = value * (KEEP / scale.astype(jnp.float32))
    q2 = q * q
    q4 = q2 * q2
    ref[d, n, :rows] = (q4 * q2 * (q * jnp.abs(q))).astype(jnp.bfloat16)
    ref[d, n, rows:] = jnp.broadcast_to(scale, (SCALE_ROWS, value.shape[1]))


def decode(ref, d, n, rows):
    code = ref[d, n, :rows].astype(jnp.float32)
    scale = ref[d, n, rows:].astype(jnp.float32)[:1]
    r1 = lax.rsqrt(jnp.maximum(jnp.abs(code), 1.2e-38))
    r2 = lax.rsqrt(r1)
    root = r2 * lax.rsqrt(r2)
    return jnp.where(code < 0, -root, root) * (scale * (1.0 / KEEP))


def kernel(nz, nc, a_ref, b_ref, r_ref, o_ref, a_all, b_all, part, send, up, dn,
           r_s, al_s, bl_s, ay_s, ay_r, ax_s, ax_r, ac_s, ac_r, by_s, by_r, z_s, up_r, dn_r):
    w, m = lax.axis_index("wide"), lax.axis_index("narrow")
    z, y, x, c = w // 2, w % 2, m // 2, m % 2
    rows, cols = r_ref.shape
    ka, kb = a_ref.shape[1], b_ref.shape[0]
    tile = cols // nc
    to_y = (z * 2 + 1 - y, m)
    to_x = (w, (1 - x) * 2 + c)
    to_c = (w, x * 2 + 1 - c)
    above, below = (w + 2, m), (w - 2, m)
    high = (2 * z) // nz

    own = z + (1 - high) * (nz - 1 - 2 * z)

    def order(i):
        last = (i + 1) // nz
        k = last * own + (1 - last) * (i + (i + nz - own) // nz)
        return k + (1 - high) * (nz - 1 - 2 * k)

    def piece(yy, xx, cc):
        return yy * 4 + xx * 2 + cc

    def rows_of(d, yy):
        return a_ref.at[pl.ds(pl.multiple_of((d * 2 + yy) * rows, rows), rows), :]

    def columns(n):
        return pl.ds(pl.multiple_of(n * tile, tile), tile)

    def remote(src, dst, s, r, to):
        return pltpu.make_async_remote_copy(
            src_ref=src, dst_ref=dst, send_sem=s, recv_sem=r, device_id=to, device_id_type=MESH)

    def a_local(i):
        d = order(i)
        return pltpu.make_async_copy(rows_of(d, y), a_all.at[d, piece(y, x, c)], al_s.at[i])

    def b_local(n):
        return pltpu.make_async_copy(
            b_ref.at[:, columns(n)], b_all.at[n, pl.ds(pl.multiple_of(y * kb, kb), kb)], bl_s.at[n])

    def a_y(i):
        d = order(i)
        return remote(rows_of(d, 1 - y), a_all.at[d, piece(y, x, c)], ay_s.at[i], ay_r.at[i], to_y)

    def a_x(i, j):
        d = order(i)
        src = rows_of(d, y) if j == 0 else a_all.at[d, piece(1 - y, x, c)]
        dst = a_all.at[d, piece(y if j == 0 else 1 - y, x, c)]
        return remote(src, dst, ax_s.at[i, j], ax_r.at[i, j], to_x)

    def a_c(i, j):
        d = order(i)
        here = piece(y if j % 2 == 0 else 1 - y, x if j < 2 else 1 - x, c)
        src = rows_of(d, y) if j == 0 else a_all.at[d, here]
        return remote(src, a_all.at[d, here], ac_s.at[i, j], ac_r.at[i, j], to_c)

    def b_y(n):
        half = b_all.at[n, pl.ds(pl.multiple_of(y * kb, kb), kb)]
        return remote(half, half, by_s.at[n], by_r.at[n], to_y)

    def c_up(d, n):
        return remote(send.at[d, n], up.at[d, n], z_s.at[d, n], up_r.at[d, n], above)

    def c_dn(d, n):
        return remote(send.at[d, n], dn.at[d, n], z_s.at[d, n], dn_r.at[d, n], below)

    residual = pltpu.make_async_copy(r_ref, o_ref, r_s)
    def product(d, n, wide=1):
        left = jnp.concatenate([a_all[d, p] for p in range(8)], axis=1)
        right = jnp.concatenate([b_all[n + k] for k in range(wide)], axis=1)
        return jnp.dot(left, right, preferred_element_type=jnp.float32)

    for n in range(nc):
        b_local(n).start()
    for i in range(nz):
        a_local(i).start()
    residual.start()

    barrier = pltpu.get_barrier_semaphore()
    for to in (to_y, to_x, to_c):
        pl.semaphore_signal(barrier, inc=1, device_id=to, device_id_type=MESH)

    @pl.when(z > 0)
    def _():
        pl.semaphore_signal(barrier, inc=1, device_id=below, device_id_type=MESH)

    @pl.when(z < nz - 1)
    def _():
        pl.semaphore_signal(barrier, inc=1, device_id=above, device_id_type=MESH)

    pl.semaphore_wait(barrier, 3 + (z + nz - 1) // nz + (2 * nz - 2 - z) // nz)

    queue = [("a", 0), ("b", 0), ("a", 1), ("b", 1), ("a", 2), ("b", 2), ("b", 3), ("b", 4), ("b", 5),
             ("b", 6), ("a", 3), ("b", 7)]

    def start_y(k):
        if k < len(queue):
            kind, e = queue[k]
            if kind == "b":
                b_local(e).wait()
            (a_y if kind == "a" else b_y)(e).start()

    def start_own(i):
        if i < nz:
            a_x(i, 0).start()
            a_c(i, 0).start()

    def a_arrives(i):
        a_y(i).wait_recv()
        start_y(queue.index(("a", i)) + AHEAD)
        a_x(i, 1).start()
        a_c(i, 1).start()
        start_own(i + 2)

    def b_arrives(n):
        b_y(n).wait_recv()
        start_y(queue.index(("b", n)) + AHEAD)

    def a_complete(i):
        a_x(i, 0).wait_recv()
        a_c(i, 2).start()
        a_x(i, 1).wait_recv()
        a_c(i, 3).start()
        a_local(i).wait()
        for j in range(4):
            a_c(i, j).wait_recv()

    for k in range(AHEAD):
        start_y(k)
    start_own(0)
    start_own(1)
    residual.wait()

    def own_product(q, carry):
        both = pl.ds(pl.multiple_of(2 * q * tile, 2 * tile), 2 * tile)
        o_ref[:, both] += product(z, 2 * q, 2)
        return carry

    def add_arrivals(n, carry):
        @pl.when(z > 0)
        def _():
            c_up(z, n).wait_recv()
            o_ref[:, columns(n)] += decode(up, z, n, rows)

        @pl.when(z < nz - 1)
        def _():
            c_dn(z, n).wait_recv()
            o_ref[:, columns(n)] += decode(dn, z, n, rows)

        return carry

    def pass_on(d, n, value):
        @pl.when(d > z)
        def _():
            @pl.when(z > 0)
            def _():
                c_up(d, n).wait_recv()
                encode(send, d, n, value[...] + decode(up, d, n, rows))

            @pl.when(z == 0)
            def _():
                encode(send, d, n, value[...])

            c_up(d, n).start()

        @pl.when(d < z)
        def _():
            @pl.when(z < nz - 1)
            def _():
                c_dn(d, n).wait_recv()
                encode(send, d, n, value[...] + decode(dn, d, n, rows))

            @pl.when(z == nz - 1)
            def _():
                encode(send, d, n, value[...])

            c_dn(d, n).start()

    def run(tiles, arrivals, wide):
        def step(t, carry):
            i, n = tiles[0]
            for k, (tile_i, tile_n) in enumerate(tiles[1:], 1):
                i = jnp.where(t == k, tile_i, i)
                n = jnp.where(t == k, tile_n, n)
            for k, arrive in arrivals.items():
                pl.when(t == k)(arrive)
            d = order(i)
            if wide == 1:
                part[0] = product(d, n)
                pass_on(d, n, part.at[0])
            else:
                both = product(d, n, 2)
                part[0] = both[:, :tile]
                part[1] = both[:, tile:]

                def half(h, carry):
                    pass_on(d, n + h, part.at[h])
                    return carry

                lax.fori_loop(0, 2, half, 0)
            return carry

        lax.fori_loop(0, len(tiles), step, 0)

    def first():
        a_arrives(0)
        b_arrives(0)
        a_complete(0)

    def second():
        a_arrives(1)
        b_arrives(1)

    def third():
        a_arrives(2)
        b_arrives(2)
        b_arrives(3)

    def fourth():
        b_arrives(4)
        b_arrives(5)

    def last():
        a_arrives(3)
        lax.fori_loop(0, 4, add_arrivals, 0)
        b_arrives(7)

    run([(0, 0), (0, 1), (1, 0), (1, 1)], {0: first, 1: second, 2: lambda: a_complete(1)}, 1)
    run([(0, 2), (1, 2), (2, 0), (2, 2), (0, 4), (1, 4), (2, 4)],
        {0: third, 2: lambda: a_complete(2), 4: fourth}, 2)
    run([(0, 6), (1, 6), (2, 6), (0, 7), (1, 7), (2, 7)], {0: lambda: b_arrives(6), 3: last}, 1)

    a_complete(3)
    lax.fori_loop(0, nc // 2, own_product, 0)
    lax.fori_loop(4, nc, add_arrivals, 0)

    def drain_a(i, carry):
        a_y(i).wait_send()
        for j in range(2):
            a_x(i, j).wait_send()
        for j in range(4):
            a_c(i, j).wait_send()
        return carry

    def drain_b(n, carry):
        b_y(n).wait_send()
        return carry

    def drain_c(t, carry):
        d, n = t // nc, t % nc

        @pl.when(d != z)
        def _():
            c_up(d, n).wait_send()

        return carry

    lax.fori_loop(0, nz, drain_a, 0)
    lax.fori_loop(0, nc, drain_b, 0)
    lax.fori_loop(0, nz * nc, drain_c, 0)


def ladder_kernel(amplitudes, integrals, old_residual):
    nz, nc = lax.axis_size("wide") // 2, CHUNKS
    rows, cols = old_residual.shape
    depth = 2 * integrals.shape[0]
    tile = cols // nc
    dma = pltpu.SemaphoreType.DMA
    return pl.pallas_call(
        functools.partial(kernel, nz, nc),
        out_shape=jax.ShapeDtypeStruct((rows, cols), jnp.float32),
        in_specs=[pl.BlockSpec(memory_space=pl.ANY)] * 3,
        out_specs=pl.BlockSpec(memory_space=pltpu.VMEM),
        scratch_shapes=[
            pltpu.VMEM((nz, 8, rows, amplitudes.shape[1]), jnp.bfloat16),
            pltpu.VMEM((nc, depth, tile), jnp.bfloat16),
            pltpu.VMEM((2, rows, tile), jnp.float32),
            pltpu.VMEM((nz, nc, rows + SCALE_ROWS, tile), jnp.bfloat16),
            pltpu.VMEM((nz, nc, rows + SCALE_ROWS, tile), jnp.bfloat16),
            pltpu.VMEM((nz, nc, rows + SCALE_ROWS, tile), jnp.bfloat16),
            dma, dma((nz,)), dma((nc,)),
            dma((nz,)), dma((nz,)),
            dma((nz, 2)), dma((nz, 2)),
            dma((nz, 4)), dma((nz, 4)),
            dma((nc,)), dma((nc,)),
            dma((nz, nc)), dma((nz, nc)), dma((nz, nc)),
        ],
        compiler_params=pltpu.CompilerParams(
            collective_id=0, has_side_effects=True, vmem_limit_bytes=52 * 1024 * 1024),
        cost_estimate=pl.CostEstimate(
            flops=2 * nz * rows * depth * cols, bytes_accessed=8 * rows * cols, transcendentals=0),
    )(amplitudes, integrals, old_residual)


def broadcast(value, axis, source):
    kept = jnp.where(lax.axis_index(axis) == source, value, 0).astype(value.dtype)
    return lax.psum(kept, axis)


def ladder_gathered(amplitudes, integrals, old_residual):
    panels = lax.axis_size("narrow")
    sub_rows = integrals.shape[0] // panels
    stacked = integrals.reshape(panels, sub_rows, integrals.shape[1])
    total = old_residual
    row_amps = lax.all_to_all(amplitudes, "wide", split_axis=0, concat_axis=1, tiled=True)
    for column in range(panels):
        panel = broadcast(row_amps, "narrow", column)
        panel_ints = lax.all_gather(stacked[column], "wide", axis=0, tiled=True)
        total = total + jnp.dot(panel, panel_ints, preferred_element_type=jnp.float32)
    return total


def per_device(amplitudes, integrals, old_residual):
    if amplitudes.shape[1] % 128 or lax.axis_size("narrow") != 4 or lax.axis_size("wide") != 8:
        return ladder_gathered(amplitudes, integrals, old_residual)
    return ladder_kernel(amplitudes, integrals, old_residual)


def solution(mesh):
    placed = (P(None, ("wide", "narrow")), P("wide", "narrow"), P("wide", "narrow"))
    return jax.shard_map(
        per_device, mesh=mesh, in_specs=placed, out_specs=P("wide", "narrow"), check_vma=False
    )
```

```python
import functools

import jax
import jax.numpy as jnp
from jax import lax
from jax.experimental import pallas as pl
from jax.experimental.pallas import tpu as pltpu
from jax.sharding import PartitionSpec as P

SCALE_ROWS = 16
KEEP = 46000.0
CHUNKS = 8
AHEAD = 3
MESH = pl.DeviceIdType.MESH


def encode(ref, d, n, value):
    rows = value.shape[0]
    peak = jnp.max(jnp.abs(value), axis=0, keepdims=True)
    scale = (peak * 1.01 + 1e-30).astype(jnp.bfloat16)
    q = value * (KEEP / scale.astype(jnp.float32))
    q2 = q * q
    q4 = q2 * q2
    ref[d, n, :rows] = (q4 * q2 * (q * jnp.abs(q))).astype(jnp.bfloat16)
    ref[d, n, rows:] = jnp.broadcast_to(scale, (SCALE_ROWS, value.shape[1]))


def decode(ref, d, n, rows):
    code = ref[d, n, :rows].astype(jnp.float32)
    scale = ref[d, n, rows:].astype(jnp.float32)[:1]
    r1 = lax.rsqrt(jnp.maximum(jnp.abs(code), 1.2e-38))
    r2 = lax.rsqrt(r1)
    root = r2 * lax.rsqrt(r2)
    return jnp.where(code < 0, -root, root) * (scale * (1.0 / KEEP))


def kernel(nz, nc, a_ref, b_ref, r_ref, o_ref, a_all, b_all, part, send, up, dn,
           r_s, al_s, bl_s, ay_s, ay_r, ax_s, ax_r, ac_s, ac_r, by_s, by_r, z_s, up_r, dn_r):
    w, m = lax.axis_index("wide"), lax.axis_index("narrow")
    z, y, x, c = w // 2, w % 2, m // 2, m % 2
    rows, cols = r_ref.shape
    ka, kb = a_ref.shape[1], b_ref.shape[0]
    tile = cols // nc
    to_y = (z * 2 + 1 - y, m)
    to_x = (w, (1 - x) * 2 + c)
    to_c = (w, x * 2 + 1 - c)
    above, below = (w + 2, m), (w - 2, m)
    high = (2 * z) // nz

    own = z + (1 - high) * (nz - 1 - 2 * z)

    def order(i):
        last = (i + 1) // nz
        k = last * own + (1 - last) * (i + (i + nz - own) // nz)
        return k + (1 - high) * (nz - 1 - 2 * k)

    def piece(yy, xx, cc):
        return pl.ds(pl.multiple_of((yy * 4 + xx * 2 + cc) * ka, ka), ka)

    def rows_of(d, yy):
        return a_ref.at[pl.ds(pl.multiple_of((d * 2 + yy) * rows, rows), rows), :]

    def columns(n):
        return pl.ds(pl.multiple_of(n * tile, tile), tile)

    def remote(src, dst, s, r, to):
        return pltpu.make_async_remote_copy(
            src_ref=src, dst_ref=dst, send_sem=s, recv_sem=r, device_id=to, device_id_type=MESH)

    def a_local(i):
        d = order(i)
        return pltpu.make_async_copy(rows_of(d, y), a_all.at[d, :, piece(y, x, c)], al_s.at[i])

    def b_local(n):
        return pltpu.make_async_copy(
            b_ref.at[:, columns(n)], b_all.at[n, pl.ds(pl.multiple_of(y * kb, kb), kb)], bl_s.at[n])

    def a_y(i):
        d = order(i)
        return remote(rows_of(d, 1 - y), a_all.at[d, :, piece(y, x, c)], ay_s.at[i], ay_r.at[i], to_y)

    def a_x(i, j):
        d = order(i)
        src = rows_of(d, y) if j == 0 else a_all.at[d, :, piece(1 - y, x, c)]
        dst = a_all.at[d, :, piece(y if j == 0 else 1 - y, x, c)]
        return remote(src, dst, ax_s.at[i, j], ax_r.at[i, j], to_x)

    def a_c(i, j):
        d = order(i)
        here = piece(y if j % 2 == 0 else 1 - y, x if j < 2 else 1 - x, c)
        src = rows_of(d, y) if j == 0 else a_all.at[d, :, here]
        return remote(src, a_all.at[d, :, here], ac_s.at[i, j], ac_r.at[i, j], to_c)

    def b_y(n):
        return remote(b_ref.at[:, columns(n)], b_all.at[n, pl.ds(pl.multiple_of(y * kb, kb), kb)],
                      by_s.at[n], by_r.at[n], to_y)

    def c_up(d, n):
        return remote(send.at[d, n], up.at[d, n], z_s.at[d, n], up_r.at[d, n], above)

    def c_dn(d, n):
        return remote(send.at[d, n], dn.at[d, n], z_s.at[d, n], dn_r.at[d, n], below)

    residual = pltpu.make_async_copy(r_ref, o_ref, r_s)
    for i in range(nz):
        a_local(i).start()
    for n in range(nc):
        b_local(n).start()
    residual.start()

    barrier = pltpu.get_barrier_semaphore()
    for to in (to_y, to_x, to_c):
        pl.semaphore_signal(barrier, inc=1, device_id=to, device_id_type=MESH)

    @pl.when(z > 0)
    def _():
        pl.semaphore_signal(barrier, inc=1, device_id=below, device_id_type=MESH)

    @pl.when(z < nz - 1)
    def _():
        pl.semaphore_signal(barrier, inc=1, device_id=above, device_id_type=MESH)

    pl.semaphore_wait(barrier, 3 + (z + nz - 1) // nz + (2 * nz - 2 - z) // nz)

    queue = []
    for e in range(nz - 1):
        queue += [("a", e), ("b", e)]
    queue += [("b", n) for n in range(nz - 1, nc - 1)] + [("a", nz - 1), ("b", nc - 1)]

    def start_y(k):
        if k < len(queue):
            (a_y if queue[k][0] == "a" else b_y)(queue[k][1]).start()

    def start_own(i):
        if i < nz:
            a_x(i, 0).start()
            a_c(i, 0).start()

    def a_arrives(i):
        a_y(i).wait_recv()
        start_y(queue.index(("a", i)) + AHEAD)
        a_x(i, 1).start()
        a_c(i, 1).start()
        start_own(i + 1)

    def b_arrives(n):
        b_local(n).wait()
        b_y(n).wait_recv()
        start_y(queue.index(("b", n)) + AHEAD)

    def a_complete(i):
        a_x(i, 0).wait_recv()
        a_c(i, 2).start()
        a_x(i, 1).wait_recv()
        a_c(i, 3).start()
        a_local(i).wait()
        for j in range(4):
            a_c(i, j).wait_recv()

    for k in range(AHEAD):
        start_y(k)
    start_own(0)
    residual.wait()

    head = [(0, 0)]
    for e in range(1, nz - 1):
        head += [(i, e) for i in range(e)] + [(e, n) for n in range(e + 1)]
    sends = (nz - 1) * nc

    def step(t, carry):
        i = (t - len(head)) % (nz - 1)
        n = nz - 1 + (t - len(head)) // (nz - 1)
        for k, (head_i, head_n) in enumerate(head):
            i = jnp.where(t == k, head_i, i)
            n = jnp.where(t == k, head_n, n)
        d = order(i)

        @pl.when(t == 0)
        def _():
            a_arrives(0)
            b_arrives(0)
            a_complete(0)

        for e in range(1, nz - 1):
            @pl.when(t == head.index((0, e)))
            def _():
                a_arrives(e)
                b_arrives(e)

            @pl.when(t == head.index((e, 0)))
            def _():
                a_complete(e)

        for e in range(nz - 1, nc):
            @pl.when(t == len(head) + (e - nz + 1) * (nz - 1))
            def _():
                if e == nc - 1:
                    a_arrives(nz - 1)
                b_arrives(e)

        part[...] = jnp.dot(a_all[d], b_all[n], preferred_element_type=jnp.float32)

        @pl.when(d > z)
        def _():
            @pl.when(z > 0)
            def _():
                c_up(d, n).wait_recv()
                encode(send, d, n, part[...] + decode(up, d, n, rows))

            @pl.when(z == 0)
            def _():
                encode(send, d, n, part[...])

            c_up(d, n).start()

        @pl.when(d < z)
        def _():
            @pl.when(z < nz - 1)
            def _():
                c_dn(d, n).wait_recv()
                encode(send, d, n, part[...] + decode(dn, d, n, rows))

            @pl.when(z == nz - 1)
            def _():
                encode(send, d, n, part[...])

            c_dn(d, n).start()

        return carry

    lax.fori_loop(0, sends, step, 0)

    a_complete(nz - 1)

    def own_product(q, carry):
        both = pl.ds(pl.multiple_of(2 * q * tile, 2 * tile), 2 * tile)
        right = jnp.concatenate([b_all[2 * q], b_all[2 * q + 1]], axis=1)
        o_ref[:, both] += jnp.dot(a_all[z], right, preferred_element_type=jnp.float32)
        return carry

    def finish(n, carry):
        @pl.when(z > 0)
        def _():
            c_up(z, n).wait_recv()
            o_ref[:, columns(n)] += decode(up, z, n, rows)

        @pl.when(z < nz - 1)
        def _():
            c_dn(z, n).wait_recv()
            o_ref[:, columns(n)] += decode(dn, z, n, rows)

        return carry

    lax.fori_loop(0, nc // 2, own_product, 0)
    lax.fori_loop(0, nc, finish, 0)

    def drain_a(i, carry):
        a_y(i).wait_send()
        for j in range(2):
            a_x(i, j).wait_send()
        for j in range(4):
            a_c(i, j).wait_send()
        return carry

    def drain_b(n, carry):
        b_y(n).wait_send()
        return carry

    def drain_c(t, carry):
        d, n = t // nc, t % nc

        @pl.when(d != z)
        def _():
            c_up(d, n).wait_send()

        return carry

    lax.fori_loop(0, nz, drain_a, 0)
    lax.fori_loop(0, nc, drain_b, 0)
    lax.fori_loop(0, nz * nc, drain_c, 0)


def ladder_kernel(amplitudes, integrals, old_residual):
    nz, nc = lax.axis_size("wide") // 2, CHUNKS
    rows, cols = old_residual.shape
    depth = 2 * integrals.shape[0]
    tile = cols // nc
    dma = pltpu.SemaphoreType.DMA
    return pl.pallas_call(
        functools.partial(kernel, nz, nc),
        out_shape=jax.ShapeDtypeStruct((rows, cols), jnp.float32),
        in_specs=[pl.BlockSpec(memory_space=pl.ANY)] * 3,
        out_specs=pl.BlockSpec(memory_space=pltpu.VMEM),
        scratch_shapes=[
            pltpu.VMEM((nz, rows, depth), jnp.bfloat16),
            pltpu.VMEM((nc, depth, tile), jnp.bfloat16),
            pltpu.VMEM((rows, tile), jnp.float32),
            pltpu.VMEM((nz, nc, rows + SCALE_ROWS, tile), jnp.bfloat16),
            pltpu.VMEM((nz, nc, rows + SCALE_ROWS, tile), jnp.bfloat16),
            pltpu.VMEM((nz, nc, rows + SCALE_ROWS, tile), jnp.bfloat16),
            dma, dma((nz,)), dma((nc,)),
            dma((nz,)), dma((nz,)),
            dma((nz, 2)), dma((nz, 2)),
            dma((nz, 4)), dma((nz, 4)),
            dma((nc,)), dma((nc,)),
            dma((nz, nc)), dma((nz, nc)), dma((nz, nc)),
        ],
        compiler_params=pltpu.CompilerParams(
            collective_id=0, has_side_effects=True, vmem_limit_bytes=52 * 1024 * 1024),
        cost_estimate=pl.CostEstimate(
            flops=2 * nz * rows * depth * cols, bytes_accessed=8 * rows * cols, transcendentals=0),
    )(amplitudes, integrals, old_residual)


def broadcast(value, axis, source):
    kept = jnp.where(lax.axis_index(axis) == source, value, 0).astype(value.dtype)
    return lax.psum(kept, axis)


def ladder_gathered(amplitudes, integrals, old_residual):
    panels = lax.axis_size("narrow")
    sub_rows = integrals.shape[0] // panels
    stacked = integrals.reshape(panels, sub_rows, integrals.shape[1])
    total = old_residual
    row_amps = lax.all_to_all(amplitudes, "wide", split_axis=0, concat_axis=1, tiled=True)
    for column in range(panels):
        panel = broadcast(row_amps, "narrow", column)
        panel_ints = lax.all_gather(stacked[column], "wide", axis=0, tiled=True)
        total = total + jnp.dot(panel, panel_ints, preferred_element_type=jnp.float32)
    return total


def per_device(amplitudes, integrals, old_residual):
    if amplitudes.shape[1] % 128 or lax.axis_size("narrow") != 4 or lax.axis_size("wide") > 8:
        return ladder_gathered(amplitudes, integrals, old_residual)
    return ladder_kernel(amplitudes, integrals, old_residual)


def solution(mesh):
    placed = (P(None, ("wide", "narrow")), P("wide", "narrow"), P("wide", "narrow"))
    return jax.shard_map(
        per_device, mesh=mesh, in_specs=placed, out_specs=P("wide", "narrow"), check_vma=False
    )
```

```python
import functools

import jax
import jax.numpy as jnp
from jax import lax
from jax.experimental import pallas as pl
from jax.experimental.pallas import tpu as pltpu
from jax.sharding import PartitionSpec as P

SCALE_ROWS = 16
KEEP = 46000.0
CHUNKS = 8
AHEAD = 3
MESH = pl.DeviceIdType.MESH


def encode(ref, d, n, value):
    rows = value.shape[0]
    peak = jnp.max(jnp.abs(value), axis=0, keepdims=True)
    scale = (peak * 1.01 + 1e-30).astype(jnp.bfloat16)
    q = value * (KEEP / scale.astype(jnp.float32))
    q2 = q * q
    q4 = q2 * q2
    ref[d, n, :rows] = (q4 * q2 * (q * jnp.abs(q))).astype(jnp.bfloat16)
    ref[d, n, rows:] = jnp.broadcast_to(scale, (SCALE_ROWS, value.shape[1]))


def decode(ref, d, n, rows):
    code = ref[d, n, :rows].astype(jnp.float32)
    scale = ref[d, n, rows:].astype(jnp.float32)[:1]
    r1 = lax.rsqrt(jnp.maximum(jnp.abs(code), 1.2e-38))
    r2 = lax.rsqrt(r1)
    root = r2 * lax.rsqrt(r2)
    return jnp.where(code < 0, -root, root) * (scale * (1.0 / KEEP))


def kernel(nz, nc, a_ref, b_ref, r_ref, o_ref, a_all, b_all, part, send, up, dn,
           r_s, al_s, bl_s, ay_s, ay_r, ax_s, ax_r, ac_s, ac_r, by_s, by_r, z_s, up_r, dn_r):
    w, m = lax.axis_index("wide"), lax.axis_index("narrow")
    z, y, x, c = w // 2, w % 2, m // 2, m % 2
    rows, cols = r_ref.shape
    ka, kb = a_ref.shape[1], b_ref.shape[0]
    tile = cols // nc
    to_y = (z * 2 + 1 - y, m)
    to_x = (w, (1 - x) * 2 + c)
    to_c = (w, x * 2 + 1 - c)
    above, below = (w + 2, m), (w - 2, m)
    high = (2 * z) // nz

    own = z + (1 - high) * (nz - 1 - 2 * z)

    def order(i):
        last = (i + 1) // nz
        k = last * own + (1 - last) * (i + (i + nz - own) // nz)
        return k + (1 - high) * (nz - 1 - 2 * k)

    def piece(yy, xx, cc):
        return pl.ds(pl.multiple_of((yy * 4 + xx * 2 + cc) * ka, ka), ka)

    def rows_of(d, yy):
        return a_ref.at[pl.ds(pl.multiple_of((d * 2 + yy) * rows, rows), rows), :]

    def columns(n):
        return pl.ds(pl.multiple_of(n * tile, tile), tile)

    def remote(src, dst, s, r, to):
        return pltpu.make_async_remote_copy(
            src_ref=src, dst_ref=dst, send_sem=s, recv_sem=r, device_id=to, device_id_type=MESH)

    def a_local(i):
        d = order(i)
        return pltpu.make_async_copy(rows_of(d, y), a_all.at[d, :, piece(y, x, c)], al_s.at[i])

    def b_local(n):
        return pltpu.make_async_copy(
            b_ref.at[:, columns(n)], b_all.at[n, pl.ds(pl.multiple_of(y * kb, kb), kb)], bl_s.at[n])

    def a_y(i):
        d = order(i)
        return remote(rows_of(d, 1 - y), a_all.at[d, :, piece(y, x, c)], ay_s.at[i], ay_r.at[i], to_y)

    def a_x(i, j):
        d = order(i)
        src = rows_of(d, y) if j == 0 else a_all.at[d, :, piece(1 - y, x, c)]
        dst = a_all.at[d, :, piece(y if j == 0 else 1 - y, x, c)]
        return remote(src, dst, ax_s.at[i, j], ax_r.at[i, j], to_x)

    def a_c(i, j):
        d = order(i)
        here = piece(y if j % 2 == 0 else 1 - y, x if j < 2 else 1 - x, c)
        src = rows_of(d, y) if j == 0 else a_all.at[d, :, here]
        return remote(src, a_all.at[d, :, here], ac_s.at[i, j], ac_r.at[i, j], to_c)

    def b_y(n):
        return remote(b_ref.at[:, columns(n)], b_all.at[n, pl.ds(pl.multiple_of(y * kb, kb), kb)],
                      by_s.at[n], by_r.at[n], to_y)

    def c_up(d, n):
        return remote(send.at[d, n], up.at[d, n], z_s.at[d, n], up_r.at[d, n], above)

    def c_dn(d, n):
        return remote(send.at[d, n], dn.at[d, n], z_s.at[d, n], dn_r.at[d, n], below)

    residual = pltpu.make_async_copy(r_ref, o_ref, r_s)
    for i in range(nz):
        a_local(i).start()
    for n in range(nc):
        b_local(n).start()
    residual.start()

    barrier = pltpu.get_barrier_semaphore()
    for to in (to_y, to_x, to_c):
        pl.semaphore_signal(barrier, inc=1, device_id=to, device_id_type=MESH)

    @pl.when(z > 0)
    def _():
        pl.semaphore_signal(barrier, inc=1, device_id=below, device_id_type=MESH)

    @pl.when(z < nz - 1)
    def _():
        pl.semaphore_signal(barrier, inc=1, device_id=above, device_id_type=MESH)

    pl.semaphore_wait(barrier, 3 + (z + nz - 1) // nz + (2 * nz - 2 - z) // nz)

    queue = []
    for e in range(nz - 1):
        queue += [("a", e), ("b", e)]
    queue += [("b", n) for n in range(nz - 1, nc)] + [("a", nz - 1)]

    def start_y(k):
        if k < len(queue):
            (a_y if queue[k][0] == "a" else b_y)(queue[k][1]).start()

    def start_own(i):
        if i < nz:
            a_x(i, 0).start()
            a_c(i, 0).start()

    def a_arrives(i):
        a_y(i).wait_recv()
        start_y(queue.index(("a", i)) + AHEAD)
        a_x(i, 1).start()
        a_c(i, 1).start()
        start_own(i + 1)

    def b_arrives(n):
        b_local(n).wait()
        b_y(n).wait_recv()
        start_y(queue.index(("b", n)) + AHEAD)

    def a_complete(i):
        a_x(i, 0).wait_recv()
        a_c(i, 2).start()
        a_x(i, 1).wait_recv()
        a_c(i, 3).start()
        a_local(i).wait()
        for j in range(4):
            a_c(i, j).wait_recv()

    for k in range(AHEAD):
        start_y(k)
    start_own(0)
    residual.wait()

    head = [(0, 0)]
    for e in range(1, nz - 1):
        head += [(i, e) for i in range(e)] + [(e, n) for n in range(e + 1)]
    sends = (nz - 1) * nc

    def step(t, carry):
        i = (t - len(head)) % (nz - 1)
        n = nz - 1 + (t - len(head)) // (nz - 1)
        for k, (head_i, head_n) in enumerate(head):
            i = jnp.where(t == k, head_i, i)
            n = jnp.where(t == k, head_n, n)
        d = order(i)

        @pl.when(t == 0)
        def _():
            a_arrives(0)
            b_arrives(0)
            a_complete(0)

        for e in range(1, nz - 1):
            @pl.when(t == head.index((0, e)))
            def _():
                a_arrives(e)
                b_arrives(e)

            @pl.when(t == head.index((e, 0)))
            def _():
                a_complete(e)

        for e in range(nz - 1, nc):
            @pl.when(t == len(head) + (e - nz + 1) * (nz - 1))
            def _():
                b_arrives(e)

        part[...] = jnp.dot(a_all[d], b_all[n], preferred_element_type=jnp.float32)

        @pl.when(d > z)
        def _():
            @pl.when(z > 0)
            def _():
                c_up(d, n).wait_recv()
                encode(send, d, n, part[...] + decode(up, d, n, rows))

            @pl.when(z == 0)
            def _():
                encode(send, d, n, part[...])

            c_up(d, n).start()

        @pl.when(d < z)
        def _():
            @pl.when(z < nz - 1)
            def _():
                c_dn(d, n).wait_recv()
                encode(send, d, n, part[...] + decode(dn, d, n, rows))

            @pl.when(z == nz - 1)
            def _():
                encode(send, d, n, part[...])

            c_dn(d, n).start()

        return carry

    lax.fori_loop(0, sends, step, 0)

    a_arrives(nz - 1)

    def own_product(q, carry):
        both = pl.ds(pl.multiple_of(2 * q * tile, 2 * tile), 2 * tile)
        right = jnp.concatenate([b_all[2 * q], b_all[2 * q + 1]], axis=1)
        o_ref[:, both] += jnp.dot(a_all[z], right, preferred_element_type=jnp.float32)
        return carry

    def finish(n, carry):
        @pl.when(z > 0)
        def _():
            c_up(z, n).wait_recv()
            o_ref[:, columns(n)] += decode(up, z, n, rows)

        @pl.when(z < nz - 1)
        def _():
            c_dn(z, n).wait_recv()
            o_ref[:, columns(n)] += decode(dn, z, n, rows)

        return carry

    lax.fori_loop(0, nc - 2, finish, 0)
    a_complete(nz - 1)
    lax.fori_loop(0, nc // 2, own_product, 0)
    lax.fori_loop(nc - 2, nc, finish, 0)

    def drain_a(i, carry):
        a_y(i).wait_send()
        for j in range(2):
            a_x(i, j).wait_send()
        for j in range(4):
            a_c(i, j).wait_send()
        return carry

    def drain_b(n, carry):
        b_y(n).wait_send()
        return carry

    def drain_c(t, carry):
        d, n = t // nc, t % nc

        @pl.when(d != z)
        def _():
            c_up(d, n).wait_send()

        return carry

    lax.fori_loop(0, nz, drain_a, 0)
    lax.fori_loop(0, nc, drain_b, 0)
    lax.fori_loop(0, nz * nc, drain_c, 0)


def ladder_kernel(amplitudes, integrals, old_residual):
    nz, nc = lax.axis_size("wide") // 2, CHUNKS
    rows, cols = old_residual.shape
    depth = 2 * integrals.shape[0]
    tile = cols // nc
    dma = pltpu.SemaphoreType.DMA
    return pl.pallas_call(
        functools.partial(kernel, nz, nc),
        out_shape=jax.ShapeDtypeStruct((rows, cols), jnp.float32),
        in_specs=[pl.BlockSpec(memory_space=pl.ANY)] * 3,
        out_specs=pl.BlockSpec(memory_space=pltpu.VMEM),
        scratch_shapes=[
            pltpu.VMEM((nz, rows, depth), jnp.bfloat16),
            pltpu.VMEM((nc, depth, tile), jnp.bfloat16),
            pltpu.VMEM((rows, tile), jnp.float32),
            pltpu.VMEM((nz, nc, rows + SCALE_ROWS, tile), jnp.bfloat16),
            pltpu.VMEM((nz, nc, rows + SCALE_ROWS, tile), jnp.bfloat16),
            pltpu.VMEM((nz, nc, rows + SCALE_ROWS, tile), jnp.bfloat16),
            dma, dma((nz,)), dma((nc,)),
            dma((nz,)), dma((nz,)),
            dma((nz, 2)), dma((nz, 2)),
            dma((nz, 4)), dma((nz, 4)),
            dma((nc,)), dma((nc,)),
            dma((nz, nc)), dma((nz, nc)), dma((nz, nc)),
        ],
        compiler_params=pltpu.CompilerParams(
            collective_id=0, has_side_effects=True, vmem_limit_bytes=52 * 1024 * 1024),
        cost_estimate=pl.CostEstimate(
            flops=2 * nz * rows * depth * cols, bytes_accessed=8 * rows * cols, transcendentals=0),
    )(amplitudes, integrals, old_residual)


def broadcast(value, axis, source):
    kept = jnp.where(lax.axis_index(axis) == source, value, 0).astype(value.dtype)
    return lax.psum(kept, axis)


def ladder_gathered(amplitudes, integrals, old_residual):
    panels = lax.axis_size("narrow")
    sub_rows = integrals.shape[0] // panels
    stacked = integrals.reshape(panels, sub_rows, integrals.shape[1])
    total = old_residual
    row_amps = lax.all_to_all(amplitudes, "wide", split_axis=0, concat_axis=1, tiled=True)
    for column in range(panels):
        panel = broadcast(row_amps, "narrow", column)
        panel_ints = lax.all_gather(stacked[column], "wide", axis=0, tiled=True)
        total = total + jnp.dot(panel, panel_ints, preferred_element_type=jnp.float32)
    return total


def per_device(amplitudes, integrals, old_residual):
    if amplitudes.shape[1] % 128 or lax.axis_size("narrow") != 4 or lax.axis_size("wide") > 8:
        return ladder_gathered(amplitudes, integrals, old_residual)
    return ladder_kernel(amplitudes, integrals, old_residual)


def solution(mesh):
    placed = (P(None, ("wide", "narrow")), P("wide", "narrow"), P("wide", "narrow"))
    return jax.shard_map(
        per_device, mesh=mesh, in_specs=placed, out_specs=P("wide", "narrow"), check_vma=False
    )
```

```python
import functools

import jax
import jax.numpy as jnp
from jax import lax
from jax.experimental import pallas as pl
from jax.experimental.pallas import tpu as pltpu
from jax.sharding import PartitionSpec as P

SCALE_ROWS = 16
KEEP = 46000.0
CHUNKS = 8
AHEAD = 3
MESH = pl.DeviceIdType.MESH


def encode(ref, d, n, value):
    rows = value.shape[0]
    peak = jnp.max(jnp.abs(value), axis=0, keepdims=True)
    scale = (peak * 1.01 + 1e-30).astype(jnp.bfloat16)
    q = value * (KEEP / scale.astype(jnp.float32))
    q2 = q * q
    q4 = q2 * q2
    ref[d, n, :rows] = (q4 * q2 * (q * jnp.abs(q))).astype(jnp.bfloat16)
    ref[d, n, rows:] = jnp.broadcast_to(scale, (SCALE_ROWS, value.shape[1]))


def decode(ref, d, n, rows):
    code = ref[d, n, :rows].astype(jnp.float32)
    scale = ref[d, n, rows:].astype(jnp.float32)[:1]
    r1 = lax.rsqrt(jnp.maximum(jnp.abs(code), 1.2e-38))
    r2 = lax.rsqrt(r1)
    root = r2 * lax.rsqrt(r2)
    return jnp.where(code < 0, -root, root) * (scale * (1.0 / KEEP))


def kernel(nz, nc, a_ref, b_ref, r_ref, o_ref, a_all, b_all, part, send, up, dn,
           r_s, al_s, bl_s, ay_s, ay_r, ax_s, ax_r, ac_s, ac_r, by_s, by_r, z_s, up_r, dn_r):
    w, m = lax.axis_index("wide"), lax.axis_index("narrow")
    z, y, x, c = w // 2, w % 2, m // 2, m % 2
    rows, cols = r_ref.shape
    ka, kb = a_ref.shape[1], b_ref.shape[0]
    tile = cols // nc
    to_y = (z * 2 + 1 - y, m)
    to_x = (w, (1 - x) * 2 + c)
    to_c = (w, x * 2 + 1 - c)
    above, below = (w + 2, m), (w - 2, m)
    high = (2 * z) // nz

    own = z + (1 - high) * (nz - 1 - 2 * z)

    def order(i):
        last = (i + 1) // nz
        k = last * own + (1 - last) * (i + (i + nz - own) // nz)
        return k + (1 - high) * (nz - 1 - 2 * k)

    def piece(yy, xx, cc):
        return pl.ds(pl.multiple_of((yy * 4 + xx * 2 + cc) * ka, ka), ka)

    def rows_of(d, yy):
        return a_ref.at[pl.ds(pl.multiple_of((d * 2 + yy) * rows, rows), rows), :]

    def columns(n):
        return pl.ds(pl.multiple_of(n * tile, tile), tile)

    def remote(src, dst, s, r, to):
        return pltpu.make_async_remote_copy(
            src_ref=src, dst_ref=dst, send_sem=s, recv_sem=r, device_id=to, device_id_type=MESH)

    def a_local(i):
        d = order(i)
        return pltpu.make_async_copy(rows_of(d, y), a_all.at[d, :, piece(y, x, c)], al_s.at[i])

    def b_local(n):
        return pltpu.make_async_copy(
            b_ref.at[:, columns(n)], b_all.at[n, pl.ds(pl.multiple_of(y * kb, kb), kb)], bl_s.at[n])

    def a_y(i):
        d = order(i)
        return remote(rows_of(d, 1 - y), a_all.at[d, :, piece(y, x, c)], ay_s.at[i], ay_r.at[i], to_y)

    def a_x(i, j):
        d = order(i)
        src = rows_of(d, y) if j == 0 else a_all.at[d, :, piece(1 - y, x, c)]
        dst = a_all.at[d, :, piece(y if j == 0 else 1 - y, x, c)]
        return remote(src, dst, ax_s.at[i, j], ax_r.at[i, j], to_x)

    def a_c(i, j):
        d = order(i)
        here = piece(y if j % 2 == 0 else 1 - y, x if j < 2 else 1 - x, c)
        src = rows_of(d, y) if j == 0 else a_all.at[d, :, here]
        return remote(src, a_all.at[d, :, here], ac_s.at[i, j], ac_r.at[i, j], to_c)

    def b_y(n):
        return remote(b_ref.at[:, columns(n)], b_all.at[n, pl.ds(pl.multiple_of(y * kb, kb), kb)],
                      by_s.at[n], by_r.at[n], to_y)

    def c_up(d, n):
        return remote(send.at[d, n], up.at[d, n], z_s.at[d, n], up_r.at[d, n], above)

    def c_dn(d, n):
        return remote(send.at[d, n], dn.at[d, n], z_s.at[d, n], dn_r.at[d, n], below)

    residual = pltpu.make_async_copy(r_ref, o_ref, r_s)
    for i in range(nz):
        a_local(i).start()
    for n in range(nc):
        b_local(n).start()
    residual.start()

    barrier = pltpu.get_barrier_semaphore()
    for to in (to_y, to_x, to_c):
        pl.semaphore_signal(barrier, inc=1, device_id=to, device_id_type=MESH)

    @pl.when(z > 0)
    def _():
        pl.semaphore_signal(barrier, inc=1, device_id=below, device_id_type=MESH)

    @pl.when(z < nz - 1)
    def _():
        pl.semaphore_signal(barrier, inc=1, device_id=above, device_id_type=MESH)

    pl.semaphore_wait(barrier, 3 + (z + nz - 1) // nz + (2 * nz - 2 - z) // nz)

    queue = [("a", 0), ("b", 0)] + [("a", e) for e in range(1, nz - 1)] + [("b", n) for n in range(1, nc - 1)]
    queue += [("a", nz - 1), ("b", nc - 1)]

    def start_y(k):
        if k < len(queue):
            (a_y if queue[k][0] == "a" else b_y)(queue[k][1]).start()

    def start_own(i):
        if i < nz:
            a_x(i, 0).start()
            a_c(i, 0).start()

    def a_arrives(i):
        a_y(i).wait_recv()
        start_y(queue.index(("a", i)) + AHEAD)
        a_x(i, 1).start()
        a_c(i, 1).start()
        start_own(i + 1)

    def b_arrives(n):
        b_local(n).wait()
        b_y(n).wait_recv()
        start_y(queue.index(("b", n)) + AHEAD)

    def a_complete(i):
        a_x(i, 0).wait_recv()
        a_c(i, 2).start()
        a_x(i, 1).wait_recv()
        a_c(i, 3).start()
        a_local(i).wait()
        for j in range(4):
            a_c(i, j).wait_recv()

    for k in range(AHEAD):
        start_y(k)
    start_own(0)
    residual.wait()

    sends = (nz - 1) * nc

    def step(t, carry):
        n, i = t // (nz - 1), t % (nz - 1)
        d = order(i)

        @pl.when(t == 0)
        def _():
            a_arrives(0)
            b_arrives(0)
            a_complete(0)

        for e in range(1, nz - 1):
            @pl.when(t == e)
            def _():
                if e == 1:
                    for later in range(1, nz - 1):
                        a_arrives(later)
                a_complete(e)

        for e in range(1, nc):
            @pl.when(t == e * (nz - 1))
            def _():
                if e == nc - 1:
                    a_arrives(nz - 1)
                b_arrives(e)

        part[...] = jnp.dot(a_all[d], b_all[n], preferred_element_type=jnp.float32)

        @pl.when(d > z)
        def _():
            @pl.when(z > 0)
            def _():
                c_up(d, n).wait_recv()
                encode(send, d, n, part[...] + decode(up, d, n, rows))

            @pl.when(z == 0)
            def _():
                encode(send, d, n, part[...])

            c_up(d, n).start()

        @pl.when(d < z)
        def _():
            @pl.when(z < nz - 1)
            def _():
                c_dn(d, n).wait_recv()
                encode(send, d, n, part[...] + decode(dn, d, n, rows))

            @pl.when(z == nz - 1)
            def _():
                encode(send, d, n, part[...])

            c_dn(d, n).start()

        return carry

    lax.fori_loop(0, sends, step, 0)

    a_complete(nz - 1)

    def own_product(q, carry):
        both = pl.ds(pl.multiple_of(2 * q * tile, 2 * tile), 2 * tile)
        right = jnp.concatenate([b_all[2 * q], b_all[2 * q + 1]], axis=1)
        o_ref[:, both] += jnp.dot(a_all[z], right, preferred_element_type=jnp.float32)
        return carry

    def finish(n, carry):
        @pl.when(z > 0)
        def _():
            c_up(z, n).wait_recv()
            o_ref[:, columns(n)] += decode(up, z, n, rows)

        @pl.when(z < nz - 1)
        def _():
            c_dn(z, n).wait_recv()
            o_ref[:, columns(n)] += decode(dn, z, n, rows)

        return carry

    lax.fori_loop(0, nc // 2, own_product, 0)
    lax.fori_loop(0, nc, finish, 0)

    def drain_a(i, carry):
        a_y(i).wait_send()
        for j in range(2):
            a_x(i, j).wait_send()
        for j in range(4):
            a_c(i, j).wait_send()
        return carry

    def drain_b(n, carry):
        b_y(n).wait_send()
        return carry

    def drain_c(t, carry):
        d, n = t // nc, t % nc

        @pl.when(d != z)
        def _():
            c_up(d, n).wait_send()

        return carry

    lax.fori_loop(0, nz, drain_a, 0)
    lax.fori_loop(0, nc, drain_b, 0)
    lax.fori_loop(0, nz * nc, drain_c, 0)


def ladder_kernel(amplitudes, integrals, old_residual):
    nz, nc = lax.axis_size("wide") // 2, CHUNKS
    rows, cols = old_residual.shape
    depth = 2 * integrals.shape[0]
    tile = cols // nc
    dma = pltpu.SemaphoreType.DMA
    return pl.pallas_call(
        functools.partial(kernel, nz, nc),
        out_shape=jax.ShapeDtypeStruct((rows, cols), jnp.float32),
        in_specs=[pl.BlockSpec(memory_space=pl.ANY)] * 3,
        out_specs=pl.BlockSpec(memory_space=pltpu.VMEM),
        scratch_shapes=[
            pltpu.VMEM((nz, rows, depth), jnp.bfloat16),
            pltpu.VMEM((nc, depth, tile), jnp.bfloat16),
            pltpu.VMEM((rows, tile), jnp.float32),
            pltpu.VMEM((nz, nc, rows + SCALE_ROWS, tile), jnp.bfloat16),
            pltpu.VMEM((nz, nc, rows + SCALE_ROWS, tile), jnp.bfloat16),
            pltpu.VMEM((nz, nc, rows + SCALE_ROWS, tile), jnp.bfloat16),
            dma, dma((nz,)), dma((nc,)),
            dma((nz,)), dma((nz,)),
            dma((nz, 2)), dma((nz, 2)),
            dma((nz, 4)), dma((nz, 4)),
            dma((nc,)), dma((nc,)),
            dma((nz, nc)), dma((nz, nc)), dma((nz, nc)),
        ],
        compiler_params=pltpu.CompilerParams(
            collective_id=0, has_side_effects=True, vmem_limit_bytes=52 * 1024 * 1024),
        cost_estimate=pl.CostEstimate(
            flops=2 * nz * rows * depth * cols, bytes_accessed=8 * rows * cols, transcendentals=0),
    )(amplitudes, integrals, old_residual)


def broadcast(value, axis, source):
    kept = jnp.where(lax.axis_index(axis) == source, value, 0).astype(value.dtype)
    return lax.psum(kept, axis)


def ladder_gathered(amplitudes, integrals, old_residual):
    panels = lax.axis_size("narrow")
    sub_rows = integrals.shape[0] // panels
    stacked = integrals.reshape(panels, sub_rows, integrals.shape[1])
    total = old_residual
    row_amps = lax.all_to_all(amplitudes, "wide", split_axis=0, concat_axis=1, tiled=True)
    for column in range(panels):
        panel = broadcast(row_amps, "narrow", column)
        panel_ints = lax.all_gather(stacked[column], "wide", axis=0, tiled=True)
        total = total + jnp.dot(panel, panel_ints, preferred_element_type=jnp.float32)
    return total


def per_device(amplitudes, integrals, old_residual):
    if amplitudes.shape[1] % 128 or lax.axis_size("narrow") != 4 or lax.axis_size("wide") > 8:
        return ladder_gathered(amplitudes, integrals, old_residual)
    return ladder_kernel(amplitudes, integrals, old_residual)


def solution(mesh):
    placed = (P(None, ("wide", "narrow")), P("wide", "narrow"), P("wide", "narrow"))
    return jax.shard_map(
        per_device, mesh=mesh, in_specs=placed, out_specs=P("wide", "narrow"), check_vma=False
    )
```

```python
import functools

import jax
import jax.numpy as jnp
from jax import lax
from jax.experimental import pallas as pl
from jax.experimental.pallas import tpu as pltpu
from jax.sharding import PartitionSpec as P

SCALE_ROWS = 16
KEEP = 46000.0
CHUNKS = 8
AHEAD = 3
MESH = pl.DeviceIdType.MESH


def encode(ref, d, n, value):
    rows = value.shape[0]
    peak = jnp.max(jnp.abs(value), axis=0, keepdims=True)
    scale = (peak * 1.01 + 1e-30).astype(jnp.bfloat16)
    q = value * (KEEP / scale.astype(jnp.float32))
    q2 = q * q
    q4 = q2 * q2
    ref[d, n, :rows] = (q4 * q2 * (q * jnp.abs(q))).astype(jnp.bfloat16)
    ref[d, n, rows:] = jnp.broadcast_to(scale, (SCALE_ROWS, value.shape[1]))


def decode(ref, d, n, rows):
    code = ref[d, n, :rows].astype(jnp.float32)
    scale = ref[d, n, rows:].astype(jnp.float32)[:1]
    r1 = lax.rsqrt(jnp.maximum(jnp.abs(code), 1.2e-38))
    r2 = lax.rsqrt(r1)
    root = r2 * lax.rsqrt(r2)
    return jnp.where(code < 0, -root, root) * (scale * (1.0 / KEEP))


def kernel(nz, nc, a_ref, b_ref, r_ref, o_ref, a_all, b_all, part, send, up, dn,
           r_s, al_s, bl_s, ay_s, ay_r, ax_s, ax_r, ac_s, ac_r, by_s, by_r, z_s, up_r, dn_r):
    w, m = lax.axis_index("wide"), lax.axis_index("narrow")
    z, y, x, c = w // 2, w % 2, m // 2, m % 2
    rows, cols = r_ref.shape
    ka, kb = a_ref.shape[1], b_ref.shape[0]
    tile = cols // nc
    to_y = (z * 2 + 1 - y, m)
    to_x = (w, (1 - x) * 2 + c)
    to_c = (w, x * 2 + 1 - c)
    above, below = (w + 2, m), (w - 2, m)
    high = (2 * z) // nz

    own = z + (1 - high) * (nz - 1 - 2 * z)

    def order(i):
        inner = (i + 2) // 3 * (1 - i // 3)
        i = i + inner * (nz - 1 - own) * (3 - 2 * i)
        last = (i + 1) // nz
        k = last * own + (1 - last) * (i + (i + nz - own) // nz)
        return k + (1 - high) * (nz - 1 - 2 * k)

    def piece(yy, xx, cc):
        return pl.ds(pl.multiple_of((yy * 4 + xx * 2 + cc) * ka, ka), ka)

    def rows_of(d, yy):
        return a_ref.at[pl.ds(pl.multiple_of((d * 2 + yy) * rows, rows), rows), :]

    def columns(n):
        return pl.ds(pl.multiple_of(n * tile, tile), tile)

    def remote(src, dst, s, r, to):
        return pltpu.make_async_remote_copy(
            src_ref=src, dst_ref=dst, send_sem=s, recv_sem=r, device_id=to, device_id_type=MESH)

    def a_local(i):
        d = order(i)
        return pltpu.make_async_copy(rows_of(d, y), a_all.at[d, :, piece(y, x, c)], al_s.at[i])

    def b_local(n):
        return pltpu.make_async_copy(
            b_ref.at[:, columns(n)], b_all.at[n, pl.ds(pl.multiple_of(y * kb, kb), kb)], bl_s.at[n])

    def a_y(i):
        d = order(i)
        return remote(rows_of(d, 1 - y), a_all.at[d, :, piece(y, x, c)], ay_s.at[i], ay_r.at[i], to_y)

    def a_x(i, j):
        d = order(i)
        src = rows_of(d, y) if j == 0 else a_all.at[d, :, piece(1 - y, x, c)]
        dst = a_all.at[d, :, piece(y if j == 0 else 1 - y, x, c)]
        return remote(src, dst, ax_s.at[i, j], ax_r.at[i, j], to_x)

    def a_c(i, j):
        d = order(i)
        here = piece(y if j % 2 == 0 else 1 - y, x if j < 2 else 1 - x, c)
        src = rows_of(d, y) if j == 0 else a_all.at[d, :, here]
        return remote(src, a_all.at[d, :, here], ac_s.at[i, j], ac_r.at[i, j], to_c)

    def b_y(n):
        return remote(b_ref.at[:, columns(n)], b_all.at[n, pl.ds(pl.multiple_of(y * kb, kb), kb)],
                      by_s.at[n], by_r.at[n], to_y)

    def c_up(d, n):
        return remote(send.at[d, n], up.at[d, n], z_s.at[d, n], up_r.at[d, n], above)

    def c_dn(d, n):
        return remote(send.at[d, n], dn.at[d, n], z_s.at[d, n], dn_r.at[d, n], below)

    residual = pltpu.make_async_copy(r_ref, o_ref, r_s)
    for i in range(nz):
        a_local(i).start()
    for n in range(nc):
        b_local(n).start()
    residual.start()

    barrier = pltpu.get_barrier_semaphore()
    for to in (to_y, to_x, to_c):
        pl.semaphore_signal(barrier, inc=1, device_id=to, device_id_type=MESH)

    @pl.when(z > 0)
    def _():
        pl.semaphore_signal(barrier, inc=1, device_id=below, device_id_type=MESH)

    @pl.when(z < nz - 1)
    def _():
        pl.semaphore_signal(barrier, inc=1, device_id=above, device_id_type=MESH)

    pl.semaphore_wait(barrier, 3 + (z + nz - 1) // nz + (2 * nz - 2 - z) // nz)

    queue = []
    for e in range(nz - 1):
        queue += [("a", e), ("b", e)]
    queue += [("b", n) for n in range(nz - 1, nc - 1)] + [("a", nz - 1), ("b", nc - 1)]

    def start_y(k):
        if k < len(queue):
            (a_y if queue[k][0] == "a" else b_y)(queue[k][1]).start()

    def start_own(i):
        if i < nz:
            a_x(i, 0).start()
            a_c(i, 0).start()

    def a_arrives(i):
        a_y(i).wait_recv()
        start_y(queue.index(("a", i)) + AHEAD)
        a_x(i, 1).start()
        a_c(i, 1).start()
        start_own(i + 1)

    def b_arrives(n):
        b_local(n).wait()
        b_y(n).wait_recv()
        start_y(queue.index(("b", n)) + AHEAD)

    def a_complete(i):
        a_x(i, 0).wait_recv()
        a_c(i, 2).start()
        a_x(i, 1).wait_recv()
        a_c(i, 3).start()
        a_local(i).wait()
        for j in range(4):
            a_c(i, j).wait_recv()

    for k in range(AHEAD):
        start_y(k)
    start_own(0)
    residual.wait()

    head = [(0, 0)]
    for e in range(1, nz - 1):
        head += [(i, e) for i in range(e)] + [(e, n) for n in range(e + 1)]
    sends = (nz - 1) * nc

    def step(t, carry):
        i = (t - len(head)) % (nz - 1)
        n = nz - 1 + (t - len(head)) // (nz - 1)
        for k, (head_i, head_n) in enumerate(head):
            i = jnp.where(t == k, head_i, i)
            n = jnp.where(t == k, head_n, n)
        d = order(i)

        @pl.when(t == 0)
        def _():
            a_arrives(0)
            b_arrives(0)
            a_complete(0)

        for e in range(1, nz - 1):
            @pl.when(t == head.index((0, e)))
            def _():
                a_arrives(e)
                b_arrives(e)

            @pl.when(t == head.index((e, 0)))
            def _():
                a_complete(e)

        for e in range(nz - 1, nc):
            @pl.when(t == len(head) + (e - nz + 1) * (nz - 1))
            def _():
                if e == nc - 1:
                    a_arrives(nz - 1)
                b_arrives(e)

        part[...] = jnp.dot(a_all[d], b_all[n], preferred_element_type=jnp.float32)

        @pl.when(d > z)
        def _():
            @pl.when(z > 0)
            def _():
                c_up(d, n).wait_recv()
                encode(send, d, n, part[...] + decode(up, d, n, rows))

            @pl.when(z == 0)
            def _():
                encode(send, d, n, part[...])

            c_up(d, n).start()

        @pl.when(d < z)
        def _():
            @pl.when(z < nz - 1)
            def _():
                c_dn(d, n).wait_recv()
                encode(send, d, n, part[...] + decode(dn, d, n, rows))

            @pl.when(z == nz - 1)
            def _():
                encode(send, d, n, part[...])

            c_dn(d, n).start()

        return carry

    lax.fori_loop(0, sends, step, 0)

    a_complete(nz - 1)

    def own_product(q, carry):
        both = pl.ds(pl.multiple_of(2 * q * tile, 2 * tile), 2 * tile)
        right = jnp.concatenate([b_all[2 * q], b_all[2 * q + 1]], axis=1)
        o_ref[:, both] += jnp.dot(a_all[z], right, preferred_element_type=jnp.float32)
        return carry

    def finish(n, carry):
        @pl.when(z > 0)
        def _():
            c_up(z, n).wait_recv()
            o_ref[:, columns(n)] += decode(up, z, n, rows)

        @pl.when(z < nz - 1)
        def _():
            c_dn(z, n).wait_recv()
            o_ref[:, columns(n)] += decode(dn, z, n, rows)

        return carry

    lax.fori_loop(0, nc // 2, own_product, 0)
    lax.fori_loop(0, nc, finish, 0)

    def drain_a(i, carry):
        a_y(i).wait_send()
        for j in range(2):
            a_x(i, j).wait_send()
        for j in range(4):
            a_c(i, j).wait_send()
        return carry

    def drain_b(n, carry):
        b_y(n).wait_send()
        return carry

    def drain_c(t, carry):
        d, n = t // nc, t % nc

        @pl.when(d != z)
        def _():
            c_up(d, n).wait_send()

        return carry

    lax.fori_loop(0, nz, drain_a, 0)
    lax.fori_loop(0, nc, drain_b, 0)
    lax.fori_loop(0, nz * nc, drain_c, 0)


def ladder_kernel(amplitudes, integrals, old_residual):
    nz, nc = lax.axis_size("wide") // 2, CHUNKS
    rows, cols = old_residual.shape
    depth = 2 * integrals.shape[0]
    tile = cols // nc
    dma = pltpu.SemaphoreType.DMA
    return pl.pallas_call(
        functools.partial(kernel, nz, nc),
        out_shape=jax.ShapeDtypeStruct((rows, cols), jnp.float32),
        in_specs=[pl.BlockSpec(memory_space=pl.ANY)] * 3,
        out_specs=pl.BlockSpec(memory_space=pltpu.VMEM),
        scratch_shapes=[
            pltpu.VMEM((nz, rows, depth), jnp.bfloat16),
            pltpu.VMEM((nc, depth, tile), jnp.bfloat16),
            pltpu.VMEM((rows, tile), jnp.float32),
            pltpu.VMEM((nz, nc, rows + SCALE_ROWS, tile), jnp.bfloat16),
            pltpu.VMEM((nz, nc, rows + SCALE_ROWS, tile), jnp.bfloat16),
            pltpu.VMEM((nz, nc, rows + SCALE_ROWS, tile), jnp.bfloat16),
            dma, dma((nz,)), dma((nc,)),
            dma((nz,)), dma((nz,)),
            dma((nz, 2)), dma((nz, 2)),
            dma((nz, 4)), dma((nz, 4)),
            dma((nc,)), dma((nc,)),
            dma((nz, nc)), dma((nz, nc)), dma((nz, nc)),
        ],
        compiler_params=pltpu.CompilerParams(
            collective_id=0, has_side_effects=True, vmem_limit_bytes=52 * 1024 * 1024),
        cost_estimate=pl.CostEstimate(
            flops=2 * nz * rows * depth * cols, bytes_accessed=8 * rows * cols, transcendentals=0),
    )(amplitudes, integrals, old_residual)


def broadcast(value, axis, source):
    kept = jnp.where(lax.axis_index(axis) == source, value, 0).astype(value.dtype)
    return lax.psum(kept, axis)


def ladder_gathered(amplitudes, integrals, old_residual):
    panels = lax.axis_size("narrow")
    sub_rows = integrals.shape[0] // panels
    stacked = integrals.reshape(panels, sub_rows, integrals.shape[1])
    total = old_residual
    row_amps = lax.all_to_all(amplitudes, "wide", split_axis=0, concat_axis=1, tiled=True)
    for column in range(panels):
        panel = broadcast(row_amps, "narrow", column)
        panel_ints = lax.all_gather(stacked[column], "wide", axis=0, tiled=True)
        total = total + jnp.dot(panel, panel_ints, preferred_element_type=jnp.float32)
    return total


def per_device(amplitudes, integrals, old_residual):
    if amplitudes.shape[1] % 128 or lax.axis_size("narrow") != 4 or lax.axis_size("wide") != 8:
        return ladder_gathered(amplitudes, integrals, old_residual)
    return ladder_kernel(amplitudes, integrals, old_residual)


def solution(mesh):
    placed = (P(None, ("wide", "narrow")), P("wide", "narrow"), P("wide", "narrow"))
    return jax.shard_map(
        per_device, mesh=mesh, in_specs=placed, out_specs=P("wide", "narrow"), check_vma=False
    )
```

```python
import functools

import jax
import jax.numpy as jnp
from jax import lax
from jax.experimental import pallas as pl
from jax.experimental.pallas import tpu as pltpu
from jax.sharding import PartitionSpec as P

SCALE_ROWS = 16
KEEP = 46000.0
CHUNKS = 8
AHEAD = 4
MESH = pl.DeviceIdType.MESH


def encode(ref, d, n, value):
    rows = value.shape[0]
    peak = jnp.max(jnp.abs(value), axis=0, keepdims=True)
    scale = (peak * 1.01 + 1e-30).astype(jnp.bfloat16)
    q = value * (KEEP / scale.astype(jnp.float32))
    q2 = q * q
    q4 = q2 * q2
    ref[d, n, :rows] = (q4 * q2 * (q * jnp.abs(q))).astype(jnp.bfloat16)
    ref[d, n, rows:] = jnp.broadcast_to(scale, (SCALE_ROWS, value.shape[1]))


def decode(ref, d, n, rows):
    code = ref[d, n, :rows].astype(jnp.float32)
    scale = ref[d, n, rows:].astype(jnp.float32)[:1]
    r1 = lax.rsqrt(jnp.maximum(jnp.abs(code), 1.2e-38))
    r2 = lax.rsqrt(r1)
    root = r2 * lax.rsqrt(r2)
    return jnp.where(code < 0, -root, root) * (scale * (1.0 / KEEP))


def kernel(nz, nc, a_ref, b_ref, r_ref, o_ref, a_all, b_all, part, send, up, dn,
           r_s, al_s, bl_s, ay_s, ay_r, ax_s, ax_r, ac_s, ac_r, by_s, by_r, z_s, up_r, dn_r):
    w, m = lax.axis_index("wide"), lax.axis_index("narrow")
    z, y, x, c = w // 2, w % 2, m // 2, m % 2
    rows, cols = r_ref.shape
    ka, kb = a_ref.shape[1], b_ref.shape[0]
    tile = cols // nc
    to_y = (z * 2 + 1 - y, m)
    to_x = (w, (1 - x) * 2 + c)
    to_c = (w, x * 2 + 1 - c)
    above, below = (w + 2, m), (w - 2, m)
    high = (2 * z) // nz

    own = z + (1 - high) * (nz - 1 - 2 * z)

    def order(i):
        last = (i + 1) // nz
        k = last * own + (1 - last) * (i + (i + nz - own) // nz)
        return k + (1 - high) * (nz - 1 - 2 * k)

    def piece(yy, xx, cc):
        return pl.ds(pl.multiple_of((yy * 4 + xx * 2 + cc) * ka, ka), ka)

    def rows_of(d, yy):
        return a_ref.at[pl.ds(pl.multiple_of((d * 2 + yy) * rows, rows), rows), :]

    def columns(n):
        return pl.ds(pl.multiple_of(n * tile, tile), tile)

    def remote(src, dst, s, r, to):
        return pltpu.make_async_remote_copy(
            src_ref=src, dst_ref=dst, send_sem=s, recv_sem=r, device_id=to, device_id_type=MESH)

    def a_local(i):
        d = order(i)
        return pltpu.make_async_copy(rows_of(d, y), a_all.at[d, :, piece(y, x, c)], al_s.at[i])

    def b_local(n):
        return pltpu.make_async_copy(
            b_ref.at[:, columns(n)], b_all.at[n, pl.ds(pl.multiple_of(y * kb, kb), kb)], bl_s.at[n])

    def a_y(i):
        d = order(i)
        return remote(rows_of(d, 1 - y), a_all.at[d, :, piece(y, x, c)], ay_s.at[i], ay_r.at[i], to_y)

    def a_x(i, j):
        d = order(i)
        src = rows_of(d, y) if j == 0 else a_all.at[d, :, piece(1 - y, x, c)]
        dst = a_all.at[d, :, piece(y if j == 0 else 1 - y, x, c)]
        return remote(src, dst, ax_s.at[i, j], ax_r.at[i, j], to_x)

    def a_c(i, j):
        d = order(i)
        here = piece(y if j % 2 == 0 else 1 - y, x if j < 2 else 1 - x, c)
        src = rows_of(d, y) if j == 0 else a_all.at[d, :, here]
        return remote(src, a_all.at[d, :, here], ac_s.at[i, j], ac_r.at[i, j], to_c)

    def b_y(n):
        return remote(b_ref.at[:, columns(n)], b_all.at[n, pl.ds(pl.multiple_of(y * kb, kb), kb)],
                      by_s.at[n], by_r.at[n], to_y)

    def c_up(d, n):
        return remote(send.at[d, n], up.at[d, n], z_s.at[d, n], up_r.at[d, n], above)

    def c_dn(d, n):
        return remote(send.at[d, n], dn.at[d, n], z_s.at[d, n], dn_r.at[d, n], below)

    residual = pltpu.make_async_copy(r_ref, o_ref, r_s)
    for i in range(nz):
        a_local(i).start()
    for n in range(nc):
        b_local(n).start()
    residual.start()

    barrier = pltpu.get_barrier_semaphore()
    for to in (to_y, to_x, to_c):
        pl.semaphore_signal(barrier, inc=1, device_id=to, device_id_type=MESH)

    @pl.when(z > 0)
    def _():
        pl.semaphore_signal(barrier, inc=1, device_id=below, device_id_type=MESH)

    @pl.when(z < nz - 1)
    def _():
        pl.semaphore_signal(barrier, inc=1, device_id=above, device_id_type=MESH)

    pl.semaphore_wait(barrier, 3 + (z + nz - 1) // nz + (2 * nz - 2 - z) // nz)

    queue = []
    for e in range(nz - 1):
        queue += [("a", e), ("b", e)]
    queue += [("b", n) for n in range(nz - 1, nc - 1)] + [("a", nz - 1), ("b", nc - 1)]

    def start_y(k):
        if k < len(queue):
            (a_y if queue[k][0] == "a" else b_y)(queue[k][1]).start()

    def start_own(i):
        if i < nz:
            a_x(i, 0).start()
            a_c(i, 0).start()

    def a_arrives(i):
        a_y(i).wait_recv()
        start_y(queue.index(("a", i)) + AHEAD)
        a_x(i, 1).start()
        a_c(i, 1).start()
        start_own(i + 1)

    def b_arrives(n):
        b_local(n).wait()
        b_y(n).wait_recv()
        start_y(queue.index(("b", n)) + AHEAD)

    def a_complete(i):
        a_x(i, 0).wait_recv()
        a_c(i, 2).start()
        a_x(i, 1).wait_recv()
        a_c(i, 3).start()
        a_local(i).wait()
        for j in range(4):
            a_c(i, j).wait_recv()

    for k in range(AHEAD):
        start_y(k)
    start_own(0)
    residual.wait()

    head = [(0, 0)]
    for e in range(1, nz - 1):
        head += [(i, e) for i in range(e)] + [(e, n) for n in range(e + 1)]
    sends = (nz - 1) * nc

    def step(t, carry):
        i = (t - len(head)) % (nz - 1)
        n = nz - 1 + (t - len(head)) // (nz - 1)
        for k, (head_i, head_n) in enumerate(head):
            i = jnp.where(t == k, head_i, i)
            n = jnp.where(t == k, head_n, n)
        d = order(i)

        @pl.when(t == 0)
        def _():
            a_arrives(0)
            b_arrives(0)
            a_complete(0)

        for e in range(1, nz - 1):
            @pl.when(t == head.index((0, e)))
            def _():
                a_arrives(e)
                b_arrives(e)

            @pl.when(t == head.index((e, 0)))
            def _():
                a_complete(e)

        for e in range(nz - 1, nc):
            @pl.when(t == len(head) + (e - nz + 1) * (nz - 1))
            def _():
                if e == nc - 1:
                    a_arrives(nz - 1)
                b_arrives(e)

        part[...] = jnp.dot(a_all[d], b_all[n], preferred_element_type=jnp.float32)

        @pl.when(d > z)
        def _():
            @pl.when(z > 0)
            def _():
                c_up(d, n).wait_recv()
                encode(send, d, n, part[...] + decode(up, d, n, rows))

            @pl.when(z == 0)
            def _():
                encode(send, d, n, part[...])

            c_up(d, n).start()

        @pl.when(d < z)
        def _():
            @pl.when(z < nz - 1)
            def _():
                c_dn(d, n).wait_recv()
                encode(send, d, n, part[...] + decode(dn, d, n, rows))

            @pl.when(z == nz - 1)
            def _():
                encode(send, d, n, part[...])

            c_dn(d, n).start()

        return carry

    lax.fori_loop(0, sends, step, 0)

    a_complete(nz - 1)

    def own_product(q, carry):
        both = pl.ds(pl.multiple_of(2 * q * tile, 2 * tile), 2 * tile)
        right = jnp.concatenate([b_all[2 * q], b_all[2 * q + 1]], axis=1)
        o_ref[:, both] += jnp.dot(a_all[z], right, preferred_element_type=jnp.float32)
        return carry

    def finish(n, carry):
        @pl.when(z > 0)
        def _():
            c_up(z, n).wait_recv()
            o_ref[:, columns(n)] += decode(up, z, n, rows)

        @pl.when(z < nz - 1)
        def _():
            c_dn(z, n).wait_recv()
            o_ref[:, columns(n)] += decode(dn, z, n, rows)

        return carry

    lax.fori_loop(0, nc // 2, own_product, 0)
    lax.fori_loop(0, nc, finish, 0)

    def drain_a(i, carry):
        a_y(i).wait_send()
        for j in range(2):
            a_x(i, j).wait_send()
        for j in range(4):
            a_c(i, j).wait_send()
        return carry

    def drain_b(n, carry):
        b_y(n).wait_send()
        return carry

    def drain_c(t, carry):
        d, n = t // nc, t % nc

        @pl.when(d != z)
        def _():
            c_up(d, n).wait_send()

        return carry

    lax.fori_loop(0, nz, drain_a, 0)
    lax.fori_loop(0, nc, drain_b, 0)
    lax.fori_loop(0, nz * nc, drain_c, 0)


def ladder_kernel(amplitudes, integrals, old_residual):
    nz, nc = lax.axis_size("wide") // 2, CHUNKS
    rows, cols = old_residual.shape
    depth = 2 * integrals.shape[0]
    tile = cols // nc
    dma = pltpu.SemaphoreType.DMA
    return pl.pallas_call(
        functools.partial(kernel, nz, nc),
        out_shape=jax.ShapeDtypeStruct((rows, cols), jnp.float32),
        in_specs=[pl.BlockSpec(memory_space=pl.ANY)] * 3,
        out_specs=pl.BlockSpec(memory_space=pltpu.VMEM),
        scratch_shapes=[
            pltpu.VMEM((nz, rows, depth), jnp.bfloat16),
            pltpu.VMEM((nc, depth, tile), jnp.bfloat16),
            pltpu.VMEM((rows, tile), jnp.float32),
            pltpu.VMEM((nz, nc, rows + SCALE_ROWS, tile), jnp.bfloat16),
            pltpu.VMEM((nz, nc, rows + SCALE_ROWS, tile), jnp.bfloat16),
            pltpu.VMEM((nz, nc, rows + SCALE_ROWS, tile), jnp.bfloat16),
            dma, dma((nz,)), dma((nc,)),
            dma((nz,)), dma((nz,)),
            dma((nz, 2)), dma((nz, 2)),
            dma((nz, 4)), dma((nz, 4)),
            dma((nc,)), dma((nc,)),
            dma((nz, nc)), dma((nz, nc)), dma((nz, nc)),
        ],
        compiler_params=pltpu.CompilerParams(
            collective_id=0, has_side_effects=True, vmem_limit_bytes=52 * 1024 * 1024),
        cost_estimate=pl.CostEstimate(
            flops=2 * nz * rows * depth * cols, bytes_accessed=8 * rows * cols, transcendentals=0),
    )(amplitudes, integrals, old_residual)


def broadcast(value, axis, source):
    kept = jnp.where(lax.axis_index(axis) == source, value, 0).astype(value.dtype)
    return lax.psum(kept, axis)


def ladder_gathered(amplitudes, integrals, old_residual):
    panels = lax.axis_size("narrow")
    sub_rows = integrals.shape[0] // panels
    stacked = integrals.reshape(panels, sub_rows, integrals.shape[1])
    total = old_residual
    row_amps = lax.all_to_all(amplitudes, "wide", split_axis=0, concat_axis=1, tiled=True)
    for column in range(panels):
        panel = broadcast(row_amps, "narrow", column)
        panel_ints = lax.all_gather(stacked[column], "wide", axis=0, tiled=True)
        total = total + jnp.dot(panel, panel_ints, preferred_element_type=jnp.float32)
    return total


def per_device(amplitudes, integrals, old_residual):
    if amplitudes.shape[1] % 128 or lax.axis_size("narrow") != 4 or lax.axis_size("wide") > 8:
        return ladder_gathered(amplitudes, integrals, old_residual)
    return ladder_kernel(amplitudes, integrals, old_residual)


def solution(mesh):
    placed = (P(None, ("wide", "narrow")), P("wide", "narrow"), P("wide", "narrow"))
    return jax.shard_map(
        per_device, mesh=mesh, in_specs=placed, out_specs=P("wide", "narrow"), check_vma=False
    )
```
